128 devices in a mesh: gx: 8 (over x, core), gy: 16 (over z, y).
Axes of the slice: x: 4, y: 4, z: 4, core: 2. Of those that a mesh axis runs over, the one named last changes fastest.
Arguments:
- positions: float32 [3, 2097152], P(None, ('gx', 'gy')), may hold values from 0.1 to 0.9
- velocity: float32 [3, 2097152], P(None, ('gx', 'gy')), may hold values from -2.5 to 2.5
- radius: float32 [2097152], P(('gx', 'gy')), may hold values from 0.3 to 0.5
- grain_mask: int32 [2097152], P(('gx', 'gy')), may hold values 0 or 1
- grain_cell: int32 [2097152], P(('gx', 'gy')), may hold values from 0 to 2047, as said below
- inner_pairs: int32 [5, 131072], P(None, ('gx', 'gy')), may hold values from -1 to 511, as said below
- cross_pairs: int32 [5, 131072], P(None, ('gx', 'gy')), may hold values from -1 to 511, as said below
- send_lists: int32 [65536], P(('gx', 'gy')), may hold values from 0 to 511
- fluid_velocity: float32 [3, 262144], P(None, ('gx', 'gy')), may hold values from -3 to 3
- pressure_grad: float32 [3, 262144], P(None, ('gx', 'gy')), may hold values from -4 to 4
Outputs:
- positions_out: float32 [3, 2097152], P(None, ('gx', 'gy'))
- velocity_out: float32 [3, 2097152], P(None, ('gx', 'gy'))
- fluid_out: float32 [3, 262144], P(None, ('gx', 'gy'))
- void_out: float32 [262144], P(('gx', 'gy'))
The draws below stay inside these ranges and needn't reach their ends.
Inputs may be any that keep to these rules, and one draw needn't show every extreme that they name: `grain_cell`: any local cell number below 2048; it names a cell of the fluid blocks of the grain's own slab, within the range of its own column. `inner_pairs`: column p belongs to DEM block p // 1024; rows 0 and 1 are two different local cluster numbers of that block; rows 2 to 4 are an offset of -1, 0 or 1 each, never all zero. `cross_pairs`: column p belongs to DEM block p // 1024; row 0 is a local cluster number, row 1 a copy slot below 512; rows 2 to 4 are an offset of -1, 0 or 1 each, never all zero.
All inputs are finite; a program needn't handle non-finite values. No bound on the sum of `grain_mask` on one device may be relied on, other than what follows from the above.
Results may differ from the reference program's by a relative error of at most 0.00014.
Values sent between devices are 32-bit elements; how exact they have to be, the bound alone decides.
No kernel may reach another device: no remote copies, remote signals or barrier semaphores. Data moves between devices by JAX's collectives and lax.ppermute only.
A program may use at most 128 MiB of HBM per device.

```python
import math
import jax
import jax.numpy as jnp
from jax import lax

SLOTS = 32
CLUSTERS_DEV = 512
GHOSTS = 64
SUBSTEPS = 2
INNER_DEV = 1024
CROSS_DEV = 1024
CELLS_DEV = 2048
GRAINS = 2097152
CELLS = 262144
INNER = 131072
CROSS = 131072
SENDS = 65536
N_GX = 8
N_GY = 16


def pair_columns(key, count, partner_range):
    part_keys = jax.random.split(key, 3)
    leading = jax.random.randint(part_keys[0], (count,), 0, CLUSTERS_DEV)
    partner = jax.random.randint(part_keys[1], (count,), 0, partner_range)
    offset_code = jax.random.randint(part_keys[2], (count,), 0, 26)
    offset_code = offset_code + (offset_code >= 13).astype(jnp.int32)
    offsets = jnp.stack([offset_code // 9 - 1, offset_code // 3 % 3 - 1, offset_code % 3 - 1])
    return (leading, partner, offsets)


def draw_inner_pairs(key, part):
    key = jax.random.fold_in(key, 3)
    leading, partner, offsets = pair_columns(key, INNER, CLUSTERS_DEV - 1)
    partner = (leading + 1 + partner) % CLUSTERS_DEV
    return jnp.concatenate([leading[None], partner[None], offsets], axis=0).astype(jnp.int32)


def draw_cross_pairs(key, part):
    key = jax.random.fold_in(key, 5)
    leading, partner, offsets = pair_columns(key, CROSS, 8 * GHOSTS)
    return jnp.concatenate([leading[None], partner[None], offsets], axis=0).astype(jnp.int32)


def draw_grain_cell(key, part):
    key = jax.random.fold_in(key, 7)
    key_pair = jax.random.split(key, 2)
    range_size = CELLS_DEV // N_GY
    column = jax.random.randint(key_pair[0], (GRAINS,), 0, N_GY)
    within = jax.random.randint(key_pair[1], (GRAINS,), 0, range_size)
    return (column * range_size + within).astype(jnp.int32)


def with_ends(values, key, low, top_value):
    longest = values.shape.index(max(values.shape))
    spots = []
    for shift in (0, 1):
        where = [jax.random.randint(jax.random.fold_in(key, axis), (), 0, length) for axis, length in enumerate(values.shape)]
        where[longest] = (where[longest] + shift) % values.shape[longest]
        spots.append(tuple(where))
    return values.at[spots[0]].set(low).at[spots[1]].set(top_value)


def block_scale(stream_key, shape, shards, least, high):
    loudness, own = 1.0, jax.random.fold_in(stream_key, 6)
    for axis_at, shards_of in shards:
        draws = jnp.exp(jax.random.uniform(jax.random.fold_in(own, axis_at), (shards_of,), jnp.float32, least / len(shards), high / len(shards)))
        loudness = loudness * jnp.repeat(draws, shape[axis_at] // shards_of).reshape([-1 if axis == axis_at else 1 for axis in range(len(shape))])
    return loudness


def normal_values(own_key, extent, width, reach, cuts=(), kind=jnp.bfloat16):
    result = width * jax.random.normal(own_key, extent, jnp.float32)
    if cuts:
        result = result * block_scale(own_key, extent, cuts, -0.22, 0.18)
    return jnp.clip(result, -reach, reach).astype(kind)


def setup_inputs(seed: int = 0) -> dict:
    seeds = jax.random.split(jax.random.key(seed), 11)
    positions = jnp.clip(0.1 + 0.79999997 * jax.random.uniform(seeds[0], (3, GRAINS), jnp.float32) ** block_scale(seeds[0], (3, GRAINS), ((1, 128),), -0.2, 0.2), 0.1, 0.9)
    velocity = normal_values(seeds[1], (3, GRAINS), 0.3, 2.5, ((1, 128),), jnp.float32)
    radius = jnp.clip(0.3 + 0.19999999 * jax.random.uniform(seeds[2], (GRAINS,), jnp.float32) ** block_scale(seeds[2], (GRAINS,), ((0, 128),), -0.2, 0.2), 0.3, 0.5)
    grain_mask = with_ends((jax.random.randint(seeds[3], (GRAINS,), 0, 5) < 4).astype(jnp.int32), jax.random.fold_in(seeds[3], 1), 0, 1)
    grain_cell = draw_grain_cell(jax.random.fold_in(seeds[10], 71), 0)
    inner_pairs = draw_inner_pairs(jax.random.fold_in(seeds[10], 71), 0)
    cross_pairs = draw_cross_pairs(jax.random.fold_in(seeds[10], 71), 0)
    send_lists = with_ends(jax.random.randint(seeds[7], (SENDS,), 0, CLUSTERS_DEV), jax.random.fold_in(seeds[7], 1), 0, CLUSTERS_DEV - 1).astype(jnp.int32)
    fluid_velocity = normal_values(seeds[8], (3, CELLS), 0.5, 3.0, ((1, 128),), jnp.float32)
    pressure_grad = normal_values(seeds[9], (3, CELLS), 1.0, 4.0, ((1, 128),), jnp.float32)
    return dict(positions=positions, velocity=velocity, radius=radius, grain_mask=grain_mask, grain_cell=grain_cell, inner_pairs=inner_pairs, cross_pairs=cross_pairs, send_lists=send_lists, fluid_velocity=fluid_velocity, pressure_grad=pressure_grad)


spring = 4.0
time_step = 0.1
grain_density = 2.65
gravity = 1.0
cell_volume = 4.0
void_floor = 0.35
drag_factor = 0.5
neighbours = [(-1, -1), (-1, 0), (-1, 1), (0, -1), (0, 1), (1, -1), (1, 0), (1, 1)]


def grain_terms(radius, grain_mask):
    weights_mask = grain_mask.astype(jnp.float32)
    sphere = (4.0 * math.pi / 3.0) * radius * radius * radius
    return weights_mask, grain_density * sphere, weights_mask * sphere


def fluid_update(totals, fluid_velocity, pressure_grad):
    void_out = jnp.maximum(1.0 - totals[0] / cell_volume, void_floor)
    drag_rate = drag_factor * (1.1 - void_out) / (void_out * void_out)
    numerator = void_out * fluid_velocity + time_step * (void_out * pressure_grad + drag_rate * totals[1:] / cell_volume)
    fluid_out = numerator / (void_out + time_step * drag_rate * totals[0] / cell_volume)
    return fluid_out, void_out, drag_rate


def contact_pairs(leading, partner, offsets):
    separation = leading[:3, :, None, :] - partner[:3, None, :, :] - offsets[:, None, None, :]
    squared = jnp.sum(separation * separation, axis=0)
    reach_sum = leading[3][:, None, :] + partner[3][None, :, :]
    weight = spring * jnp.maximum(reach_sum * reach_sum - squared, 0.0) * leading[4][:, None, :] * partner[4][None, :, :]
    pushes = weight[None] * separation
    return jnp.sum(pushes, axis=2), -jnp.sum(pushes, axis=1)


def cluster_forces(own_clusters, ghosts, inner_list, cross_list):
    leading = jnp.take(own_clusters, inner_list[0], axis=2)
    partner = jnp.take(own_clusters, inner_list[1], axis=2)
    on_leading, on_partner = contact_pairs(leading, partner, inner_list[2:5].astype(jnp.float32))
    forces = jnp.zeros((3,) + own_clusters.shape[1:], jnp.float32)
    forces = forces.at[:, :, inner_list[0]].add(on_leading).at[:, :, inner_list[1]].add(on_partner)
    leading = jnp.take(own_clusters, cross_list[0], axis=2)
    partner = jnp.take(ghosts, cross_list[1], axis=2)
    on_leading, on_partner = contact_pairs(leading, partner, cross_list[2:5].astype(jnp.float32))
    forces = forces.at[:, :, cross_list[0]].add(on_leading)
    reactions = jnp.zeros((3,) + ghosts.shape[1:], jnp.float32).at[:, :, cross_list[1]].add(on_partner)
    return forces, reactions


def advance(positions, velocity, contact, grain_fluid, grain_drag, weights_mask, masses, volumes):
    upward = jnp.array([0.0, 0.0, 1.0], jnp.float32)[:, None]
    drag_pull = grain_drag * volumes * (grain_fluid - velocity)
    velocity = velocity + time_step * weights_mask * ((contact + drag_pull) / masses - gravity * upward)
    positions = positions + time_step * weights_mask * velocity
    return positions, velocity


def reference(positions, velocity, radius, grain_mask, grain_cell, inner_pairs, cross_pairs, send_lists, fluid_velocity, pressure_grad):
    blocks = N_GX * N_GY
    weights_mask, masses, volumes = grain_terms(radius, grain_mask)
    grain_ids = jnp.arange(GRAINS, dtype=jnp.int32)
    owners = grain_ids // (CLUSTERS_DEV * SLOTS)
    owner_x = owners // N_GY
    owner_y = owners % N_GY
    range_size = CELLS_DEV // N_GY
    cell_index = (owner_x * (N_GY * CELLS_DEV) + (grain_cell // range_size) * CELLS_DEV + owner_y * range_size + grain_cell % range_size).astype(jnp.int32)
    deposits = jnp.concatenate([volumes[None], volumes[None] * velocity], axis=0)
    totals = jnp.zeros((4, CELLS), jnp.float32).at[:, cell_index].add(deposits)
    fluid_out, void_out, drag_rate = fluid_update(totals, fluid_velocity, pressure_grad)
    grain_fluid = fluid_out[:, cell_index]
    grain_drag = drag_rate[cell_index]
    block_ids = jnp.arange(blocks, dtype=jnp.int32)
    block_x = block_ids // N_GY
    block_y = block_ids % N_GY
    outbound = send_lists.reshape(blocks, 8, GHOSTS)
    inner_all = inner_pairs.reshape(5, blocks, INNER_DEV).transpose(1, 0, 2)
    cross_all = cross_pairs.reshape(5, blocks, CROSS_DEV).transpose(1, 0, 2)
    sources = []
    for slot_index, (step_x, step_y) in enumerate(neighbours):
        source_x = block_x + step_x
        source_y = block_y + step_y
        present = (source_x >= 0) & (source_x < N_GX) & (source_y >= 0) & (source_y < N_GY)
        source = jnp.clip(source_x, 0, N_GX - 1) * N_GY + jnp.clip(source_y, 0, N_GY - 1)
        target = (source[:, None] * CLUSTERS_DEV + outbound[source, 7 - slot_index]).astype(jnp.int32)
        sources.append((target, present.astype(jnp.float32)))

    def one_block(items):
        own_clusters, ghost_block, inner_list, cross_list = items
        return cluster_forces(own_clusters, ghost_block, inner_list, cross_list)

    for substep in range(SUBSTEPS):
        packed = jnp.concatenate([positions, radius[None], weights_mask[None]], axis=0)
        clusters = packed.reshape(5, blocks * CLUSTERS_DEV, SLOTS).transpose(0, 2, 1)
        ghost_parts = [jnp.take(clusters, target, axis=2) * present[:, None] for target, present in sources]
        ghosts = jnp.stack(ghost_parts, axis=3).reshape(5, SLOTS, blocks, 8 * GHOSTS)
        local_all = clusters.reshape(5, SLOTS, blocks, CLUSTERS_DEV).transpose(2, 0, 1, 3)
        forces, reactions = lax.map(one_block, (local_all, ghosts.transpose(2, 0, 1, 3), inner_all, cross_all))
        merged = forces.transpose(1, 2, 0, 3).reshape(3, SLOTS, blocks * CLUSTERS_DEV)
        pieces_back = reactions.reshape(blocks, 3, SLOTS, 8, GHOSTS)
        for slot_index, (target, present) in enumerate(sources):
            merged = merged.at[:, :, target].add(pieces_back[:, :, :, slot_index].transpose(1, 2, 0, 3) * present[:, None])
        contact = merged.transpose(0, 2, 1).reshape(3, GRAINS)
        positions, velocity = advance(positions, velocity, contact, grain_fluid, grain_drag, weights_mask, masses, volumes)
    return positions, velocity, fluid_out, void_out
```

```python
import math

import jax
import jax.numpy as jnp
from jax import lax
from jax.experimental import pallas as pl
from jax.experimental.pallas import tpu as pltpu
from jax.sharding import PartitionSpec as P

SLOTS = 32
LANES = 128
CLUSTERS = 512
GHOSTS = 64
PAIRS = 1024
CHUNKS = 128
GROUP = 4
NEIGHBOURS = ((-1, -1), (-1, 0), (-1, 1), (0, -1), (0, 1), (1, -1), (1, 0), (1, 1))
GHOST_ORDER = (7, 2, 3, 4, 5, 0, 1, 6)
FAR = 2.0**30

spring = 4.0
time_step = 0.1
grain_density = 2.65
gravity = 1.0
cell_volume = 4.0
void_floor = 0.35
drag_factor = 0.5

f32 = jnp.float32
bf16 = jnp.bfloat16
PARAMS = pltpu.CompilerParams(vmem_limit_bytes=24 * 1024 * 1024)


def split(values, parts):
    pieces = []
    for _ in range(parts - 1):
        piece = values.astype(bf16)
        pieces.append(piece)
        values = values - piece.astype(f32)
    pieces.append(values.astype(bf16))
    return pieces


def one_hot(index_row, count):
    rows = lax.broadcasted_iota(jnp.int32, (count, index_row.shape[1]), 0)
    return jnp.where(rows == index_row, 1.0, 0.0).astype(bf16)


def dot(left, right):
    return jnp.dot(left, right, preferred_element_type=f32)


def dot_lanes(left, right):
    return lax.dot_general(left, right, (((1,), (1,)), ((), ())), preferred_element_type=f32)


def cluster_column(index):
    return (index & (GROUP - 1)) * LANES + (index >> 2)


def ghost_column(slot):
    block = slot >> 6
    column = jnp.zeros_like(slot)
    for position, offset in enumerate(GHOST_ORDER):
        column = jnp.where(block == offset, position * GHOSTS, column)
    return column + (slot & (GHOSTS - 1))


def lower_half(shape):
    return lax.broadcasted_iota(jnp.int32, shape, 1) < GHOSTS


def to_table(square):
    turned = square.T
    return jnp.concatenate([turned[k * SLOTS : (k + 1) * SLOTS] for k in range(GROUP)], axis=1)


def from_table(table):
    stacked = jnp.concatenate([table[:, k * LANES : (k + 1) * LANES] for k in range(GROUP)], axis=0)
    return stacked.T


def load_components(ref, stage):
    for i in range(CHUNKS):
        stage[pl.ds(i, 3, stride=CHUNKS), :] = ref[:, i * LANES : (i + 1) * LANES]
    return [to_table(stage[c * CHUNKS : (c + 1) * CHUNKS, :]) for c in range(3)]


def store_components(ref, stage, table):
    for c in range(3):
        stage[c * CHUNKS : (c + 1) * CHUNKS, :] = from_table(table[c * SLOTS : (c + 1) * SLOTS])
    for i in range(CHUNKS):
        ref[:, i * LANES : (i + 1) * LANES] = stage[pl.ds(i, 3, stride=CHUNKS), :]


def gather(table_parts, hot, rows):
    picked = dot(table_parts, hot)
    total = picked[:rows]
    for k in range(1, table_parts.shape[0] // rows):
        total = total + picked[k * rows : (k + 1) * rows]
    return total


def send_pieces(table, rows, send_ref, first_ref, second_ref):
    parts = jnp.concatenate(split(table[:rows], 3), axis=0)
    half = CLUSTERS // 2
    for k, out in enumerate((first_ref, second_ref)):
        hot = one_hot(cluster_column(send_ref[:, k * half : (k + 1) * half]), CLUSTERS)
        out[...] = gather(parts, hot, rows)


def prepare(positions, radius, mask, send, table_out, state_out, first, second, stage):
    parts = load_components(positions, stage)
    reach = to_table(radius[...])
    weights = to_table(mask[...].astype(f32))
    real = weights > 0.5
    table = jnp.concatenate([jnp.where(real, part, FAR) for part in parts] + [reach], axis=0)
    table_out[...] = table
    for c in range(3):
        state_out[c * SLOTS : (c + 1) * SLOTS] = parts[c]
    state_out[3 * SLOTS :] = weights
    send_pieces(table, 4 * SLOTS, send, first, second)


def contacts(leading, partner, on_leading, on_partner):
    on_partner[...] = jnp.zeros_like(on_partner)
    step = 4

    def row(component, slot):
        return pl.ds(pl.multiple_of((component * SLOTS + slot) * 8, 8), 8)

    def some_slots(block, carry):
        base = block * step
        ours = [[leading[row(c, base + i), :] for c in range(4)] for i in range(step)]
        sums = [[jnp.zeros((8, LANES), f32) for _ in range(3)] for _ in range(step)]
        for q in range(SLOTS):
            theirs = [partner[row(c, q), :] for c in range(4)]
            back = [on_partner[row(c, q), :] for c in range(3)]
            for i in range(step):
                apart = [ours[i][c] - theirs[c] for c in range(3)]
                squared = apart[0] * apart[0] + apart[1] * apart[1] + apart[2] * apart[2]
                reach = ours[i][3] + theirs[3]
                weight = jnp.maximum(reach * reach - squared, 0.0)
                for c in range(3):
                    push = weight * apart[c]
                    sums[i][c] = sums[i][c] + push
                    back[c] = back[c] + push
            for c in range(3):
                on_partner[row(c, q), :] = back[c]
        for i in range(step):
            for c in range(3):
                on_leading[row(c, base + i), :] = sums[i][c]
        return carry

    lax.fori_loop(0, SLOTS // step, some_slots, 0)


def pair_sums(pairs, leading_parts, partner_parts, partner_column, scratch):
    hot_a, hot_b, leading, partner, on_leading, on_partner = scratch
    width = 2 * LANES
    for block in range(PAIRS // width):
        span = slice(block * width, (block + 1) * width)
        for row, column, parts, hot, landed in (
            (0, cluster_column, leading_parts, hot_a, leading),
            (1, partner_column, partner_parts, hot_b, partner),
        ):
            chosen = one_hot(column(pairs[row : row + 1, span]), CLUSTERS)
            hot[:, span] = chosen
            picked = gather(parts, chosen, 4 * SLOTS)
            if row == 0:
                offsets = pairs[2:5, span].astype(f32)
                picked = jnp.concatenate(
                    [picked[c * SLOTS : (c + 1) * SLOTS] - offsets[c : c + 1] for c in range(3)]
                    + [picked[3 * SLOTS :]],
                    axis=0,
                )
            for k in range(2):
                landed[pl.ds(2 * block + k, 4 * SLOTS, stride=8), :] = picked[
                    :, k * LANES : (k + 1) * LANES
                ]
    contacts(leading, partner, on_leading, on_partner)
    totals = []
    for sums, hot in ((on_leading, hot_a), (on_partner, hot_b)):
        pieces = jnp.concatenate(
            [sums[pl.ds(k, 3 * SLOTS, stride=8), :] for k in range(PAIRS // LANES)], axis=1
        )
        added = dot_lanes(jnp.concatenate(split(pieces, 2), axis=0), hot[...])
        totals.append(added[: 3 * SLOTS] + added[3 * SLOTS :])
    return totals


def inner_kernel(table, pairs, force, *scratch):
    parts = jnp.concatenate(split(table[...], 3), axis=0)
    on_leading, on_partner = pair_sums(pairs, parts, parts, cluster_column, scratch)
    force[...] = on_leading - on_partner


def present_tile(low, high):
    here_x, here_y = lax.axis_index("gx"), lax.axis_index("gy")
    flags = []
    for slot in (low, high):
        a, b = NEIGHBOURS[slot]
        x, y = here_x + a, here_y + b
        inside = (x >= 0) & (x < lax.axis_size("gx")) & (y >= 0) & (y < lax.axis_size("gy"))
        flags.append(jnp.where(inside, 1, 0))
    return jnp.where(lower_half((1, LANES)), flags[0], flags[1]) > 0


def cross_kernel(
    table, pairs, reach, below, above, from_next, from_last, force, up, down, keep, reach_out, *scratch
):
    rows = below.shape[0]
    low = lower_half((rows, LANES))
    tiles = [
        below[:, :LANES],
        jnp.where(low, above[:, LANES:], below[:, LANES:]),
        above[:, :LANES],
        jnp.where(low, from_last[:, LANES:], from_next[:, :LANES]),
    ]
    for k in range(4):
        there = present_tile(GHOST_ORDER[2 * k], GHOST_ORDER[2 * k + 1])
        placed = jnp.where(there, tiles[k][: 3 * SLOTS], FAR)
        size = reach[:, k * LANES : (k + 1) * LANES] if rows == 3 * SLOTS else tiles[k][3 * SLOTS :]
        reach_out[:, k * LANES : (k + 1) * LANES] = size
        tiles[k] = jnp.concatenate([placed, size], axis=0)
    ghosts = jnp.concatenate(tiles, axis=1)
    own_parts = jnp.concatenate(split(table[...], 3), axis=0)
    ghost_parts = jnp.concatenate(split(ghosts, 3), axis=0)
    on_leading, on_partner = pair_sums(pairs, own_parts, ghost_parts, ghost_column, scratch)
    force[...] = on_leading
    up[...] = on_partner[:, : 2 * LANES]
    down[...] = on_partner[:, LANES : 3 * LANES]
    keep[...] = on_partner[:, 3 * LANES :]


def deposit_kernel(velocity, radius, mask, cell, velocity_out, cell_out, totals, stage):
    parts = load_components(velocity, stage)
    reach = to_table(radius[...])
    weights = to_table(mask[...].astype(f32))
    cells = to_table(cell[...].astype(f32)).astype(jnp.int32)
    volumes = weights * ((4.0 * math.pi / 3.0) * reach * reach * reach)
    for c in range(3):
        velocity_out[c * SLOTS : (c + 1) * SLOTS] = parts[c]
    cell_out[...] = cells
    amounts = [volumes] + [volumes * part for part in parts]
    total = jnp.zeros((2 * 4 * 16, LANES), f32)
    for slot in range(SLOTS):
        cell_row = cells[slot : slot + 1]
        hot = one_hot(cell_row & (LANES - 1), LANES)
        group = lax.broadcasted_iota(jnp.int32, (16, CLUSTERS), 0) == (cell_row >> 7)
        spread = jnp.concatenate(
            [jnp.where(group, amount[slot : slot + 1], 0.0) for amount in amounts], axis=0
        )
        total = total + dot_lanes(jnp.concatenate(split(spread, 2), axis=0), hot)
    totals[...] = total[:64] + total[64:]


def fluid_kernel(totals, fluid, cell, fields_out, at_grain):
    volume = totals[:16]
    void_out = jnp.maximum(1.0 - volume / cell_volume, void_floor)
    drag_rate = drag_factor * (1.1 - void_out) / (void_out * void_out)
    below = void_out + time_step * drag_rate * volume / cell_volume
    fields = []
    for c in range(3):
        push = void_out * fluid[c + 3] + drag_rate * totals[(c + 1) * 16 : (c + 2) * 16] / cell_volume
        fields.append((void_out * fluid[c] + time_step * push) / below)
        fields_out[c] = fields[c]
    fields_out[3] = void_out
    fields.append(drag_rate)
    parts = jnp.concatenate(split(jnp.concatenate(fields, axis=0), 2), axis=1)
    for slot in range(SLOTS):
        cell_row = cell[slot : slot + 1, :]
        hot = one_hot(cell_row & (LANES - 1), LANES)
        seen = dot(parts, jnp.concatenate([hot, hot], axis=0))
        group = lax.broadcasted_iota(jnp.int32, (16, CLUSTERS), 0) == (cell_row >> 7)
        for c in range(4):
            chosen = jnp.where(group, seen[c * 16 : (c + 1) * 16], 0.0)
            row = c * SLOTS + slot
            at_grain[row : row + 1, :] = jnp.sum(chosen, axis=0, keepdims=True)


def advance(state, velocity, reach, at_grain, inner, cross, above, below, from_last, from_next, send):
    low = lower_half((3 * SLOTS, LANES))
    tiles = [
        from_last[:, :LANES],
        jnp.where(low, from_last[:, LANES:], below[:, LANES:]),
        jnp.where(low, above[:, :LANES], from_next[:, :LANES]),
        from_next[:, LANES:],
    ]
    tiles = [jnp.where(present_tile(2 * k, 2 * k + 1), tiles[k], 0.0) for k in range(4)]
    returned = jnp.concatenate(tiles, axis=1)
    hot = one_hot(cluster_column(send[...]), CLUSTERS)
    added = dot_lanes(jnp.concatenate(split(returned, 2), axis=0), hot)
    contact = spring * (inner[...] + cross[...] - (added[: 3 * SLOTS] + added[3 * SLOTS :]))
    weights = state[3 * SLOTS :, :]
    sphere = (4.0 * math.pi / 3.0) * reach * reach * reach
    masses = grain_density * sphere
    volumes = weights * sphere
    drag = at_grain[3 * SLOTS :, :] * volumes
    places, speeds = [], []
    for c in range(3):
        rows = slice(c * SLOTS, (c + 1) * SLOTS)
        speed = velocity[rows, :]
        pull = (contact[rows] + drag * (at_grain[rows, :] - speed)) / masses
        if c == 2:
            pull = pull - gravity
        speed = speed + time_step * weights * pull
        speeds.append(speed)
        places.append(state[rows, :] + time_step * weights * speed)
    return places, speeds, weights


def middle_kernel(
    table, state, velocity, at_grain, inner, cross, above, below, from_last, from_next, send,
    table_out, state_out, velocity_out, first, second,
):
    reach = table[3 * SLOTS :, :]
    places, speeds, weights = advance(
        state, velocity, reach, at_grain, inner, cross, above, below, from_last, from_next, send
    )
    real = weights > 0.5
    moved = jnp.concatenate([jnp.where(real, place, FAR) for place in places] + [reach], axis=0)
    table_out[...] = moved
    for c in range(3):
        state_out[c * SLOTS : (c + 1) * SLOTS] = places[c]
        velocity_out[c * SLOTS : (c + 1) * SLOTS] = speeds[c]
    state_out[3 * SLOTS :] = weights
    send_pieces(moved, 3 * SLOTS, send, first, second)


def last_kernel(
    table, state, velocity, at_grain, inner, cross, above, below, from_last, from_next, send,
    positions_out, velocity_out, stage,
):
    places, speeds, _ = advance(
        state, velocity, table[3 * SLOTS :, :], at_grain, inner, cross, above, below, from_last,
        from_next, send,
    )
    store_components(positions_out, stage, jnp.concatenate(places, axis=0))
    store_components(velocity_out, stage, jnp.concatenate(speeds, axis=0))


def shift(array, step_x, step_y):
    size_x, size_y = lax.axis_size("gx"), lax.axis_size("gy")
    moves = []
    for x in range(size_x):
        for y in range(size_y):
            target = (x + step_x) % size_x * size_y + (y + step_y) % size_y
            moves.append((x * size_y + y, target))
    return lax.ppermute(array, ("gx", "gy"), moves)


def halves(low_from, high_from):
    return jnp.where(lower_half(low_from.shape), low_from, high_from)


def spread_ghosts(first, second):
    from_next = shift(first, -1, 0)
    from_last = shift(second, 1, 0)
    minus = jnp.concatenate(
        [halves(from_next[:, :LANES], from_last[:, :LANES]), first[:, LANES:]], axis=1
    )
    plus = jnp.concatenate(
        [halves(from_next[:, LANES:], from_last[:, LANES:]), second[:, :LANES]], axis=1
    )
    return shift(minus, 0, -1), shift(plus, 0, 1), from_next, from_last


def return_forces(up, down, keep):
    below = shift(up, 0, 1)
    above = shift(down, 0, -1)
    first = jnp.concatenate([halves(below[:, :LANES], keep), above[:, LANES:]], axis=1)
    second = jnp.concatenate([below[:, :LANES], halves(keep, above[:, LANES:])], axis=1)
    return above, below, shift(first, 1, 0), shift(second, -1, 0)


def table_shape(rows, columns=CLUSTERS):
    return jax.ShapeDtypeStruct((rows, columns), f32)


STAGE = [pltpu.VMEM((3 * CHUNKS, LANES), f32)]
PAIR_SCRATCH = [
    pltpu.VMEM((CLUSTERS, PAIRS), bf16),
    pltpu.VMEM((CLUSTERS, PAIRS), bf16),
    pltpu.VMEM((4 * SLOTS * 8, LANES), f32),
    pltpu.VMEM((4 * SLOTS * 8, LANES), f32),
    pltpu.VMEM((3 * SLOTS * 8, LANES), f32),
    pltpu.VMEM((3 * SLOTS * 8, LANES), f32),
]


def call(kernel, out_shape, operands, scratch=(), cost=0):
    return pl.pallas_call(
        kernel,
        out_shape=out_shape,
        scratch_shapes=list(scratch),
        compiler_params=PARAMS,
        cost_estimate=pl.CostEstimate(flops=cost, bytes_accessed=cost // 200, transcendentals=0),
        name=kernel.__name__,
    )(*operands)


def shards(
    positions,
    velocity,
    radius,
    grain_mask,
    grain_cell,
    inner_pairs,
    cross_pairs,
    send_lists,
    fluid_velocity,
    pressure_grad,
):
    send = send_lists.reshape(1, -1)
    radius = radius.reshape(CHUNKS, LANES)
    mask = grain_mask.reshape(CHUNKS, LANES)
    cell = grain_cell.reshape(CHUNKS, LANES)
    column_here = lax.axis_index("gy")
    fluid = lax.all_gather(jnp.concatenate([fluid_velocity, pressure_grad], axis=0), "gy", axis=0)
    fluid = lax.dynamic_slice_in_dim(fluid, column_here * LANES, LANES, 2).transpose(1, 0, 2)

    full, wide = table_shape(4 * SLOTS), table_shape(4 * SLOTS, 2 * LANES)
    narrow = table_shape(3 * SLOTS, 2 * LANES)
    three = table_shape(3 * SLOTS)
    table, state, first, second = call(
        prepare, (full, full, wide, wide), (positions, radius, mask, send), STAGE, 10**9
    )
    moving, cells, totals = call(
        deposit_kernel,
        (three, jax.ShapeDtypeStruct((SLOTS, CLUSTERS), jnp.int32), table_shape(64, LANES)),
        (velocity, radius, mask, cell),
        STAGE,
        2 * 10**9,
    )
    fields, at_grain = call(
        fluid_kernel,
        (jax.ShapeDtypeStruct((4, 16, LANES), f32), full),
        (totals, fluid, cells),
        (),
        2 * 10**9,
    )
    spread = lax.all_gather(fields, "gy", axis=0)
    owned = lax.dynamic_index_in_dim(spread, column_here, 2, keepdims=False)
    owned = owned.transpose(1, 0, 2).reshape(4, -1)

    reach = table_shape(SLOTS)
    ghost_reach = jnp.zeros((SLOTS, CLUSTERS), f32)
    for substep in range(2):
        below, above, from_next, from_last = spread_ghosts(first, second)
        inner = call(inner_kernel, three, (table, inner_pairs), PAIR_SCRATCH, 4 * 10**9)
        cross, up, down, keep, new_reach = call(
            cross_kernel,
            (three, narrow, narrow, table_shape(3 * SLOTS, LANES), reach),
            (table, cross_pairs, ghost_reach, below, above, from_next, from_last),
            PAIR_SCRATCH,
            4 * 10**9,
        )
        above, below, from_last, from_next = return_forces(up, down, keep)
        operands = (
            table, state, moving, at_grain, inner, cross, above, below, from_last, from_next, send
        )
        if substep == 0:
            ghost_reach = new_reach
            table, state, moving, first, second = call(
                middle_kernel, (full, full, three, narrow, narrow), operands, (), 10**9
            )
        else:
            shape = jax.ShapeDtypeStruct(positions.shape, f32)
            positions, velocity = call(last_kernel, (shape, shape), operands, STAGE, 10**9)
    return positions, velocity, owned[:3], owned[3]


def solution(mesh):
    placed = (
        P(None, ("gx", "gy")),
        P(None, ("gx", "gy")),
        P(("gx", "gy")),
        P(("gx", "gy")),
        P(("gx", "gy")),
        P(None, ("gx", "gy")),
        P(None, ("gx", "gy")),
        P(("gx", "gy")),
        P(None, ("gx", "gy")),
        P(None, ("gx", "gy")),
    )
    return jax.shard_map(
        shards,
        mesh=mesh,
        in_specs=placed,
        out_specs=(
            P(None, ("gx", "gy")),
            P(None, ("gx", "gy")),
            P(None, ("gx", "gy")),
            P(("gx", "gy")),
        ),
        check_vma=False,
    )
```

```python
import math

import jax
import jax.numpy as jnp
from jax import lax
from jax.experimental import pallas as pl
from jax.experimental.pallas import tpu as pltpu
from jax.sharding import PartitionSpec as P

SLOTS = 32
LANES = 128
CLUSTERS = 512
GHOSTS = 64
PAIRS = 1024
CHUNKS = 128
GROUP = 4
NEIGHBOURS = ((-1, -1), (-1, 0), (-1, 1), (0, -1), (0, 1), (1, -1), (1, 0), (1, 1))
GHOST_ORDER = (7, 2, 3, 4, 5, 0, 1, 6)
FAR = 2.0**30

spring = 4.0
time_step = 0.1
grain_density = 2.65
gravity = 1.0
cell_volume = 4.0
void_floor = 0.35
drag_factor = 0.5

f32 = jnp.float32
bf16 = jnp.bfloat16
PARAMS = pltpu.CompilerParams(vmem_limit_bytes=24 * 1024 * 1024)


def split(values, parts):
    pieces = []
    for _ in range(parts - 1):
        piece = values.astype(bf16)
        pieces.append(piece)
        values = values - piece.astype(f32)
    pieces.append(values.astype(bf16))
    return pieces


def one_hot(index_row, count):
    rows = lax.broadcasted_iota(jnp.int32, (count, index_row.shape[1]), 0)
    return jnp.where(rows == index_row, 1.0, 0.0).astype(bf16)


def dot(left, right):
    return jnp.dot(left, right, preferred_element_type=f32)


def dot_lanes(left, right):
    return lax.dot_general(left, right, (((1,), (1,)), ((), ())), preferred_element_type=f32)


def cluster_column(index):
    return (index & (GROUP - 1)) * LANES + (index >> 2)


def ghost_column(slot):
    block = slot >> 6
    column = jnp.zeros_like(slot)
    for position, offset in enumerate(GHOST_ORDER):
        column = jnp.where(block == offset, position * GHOSTS, column)
    return column + (slot & (GHOSTS - 1))


def lower_half(shape):
    return lax.broadcasted_iota(jnp.int32, shape, 1) < GHOSTS


def to_table(square):
    turned = square.T
    return jnp.concatenate([turned[k * SLOTS : (k + 1) * SLOTS] for k in range(GROUP)], axis=1)


def from_table(table):
    stacked = jnp.concatenate([table[:, k * LANES : (k + 1) * LANES] for k in range(GROUP)], axis=0)
    return stacked.T


def load_components(ref, stage):
    for i in range(CHUNKS):
        stage[pl.ds(i, 3, stride=CHUNKS), :] = ref[:, i * LANES : (i + 1) * LANES]
    return [to_table(stage[c * CHUNKS : (c + 1) * CHUNKS, :]) for c in range(3)]


def store_components(ref, stage, table):
    for c in range(3):
        stage[c * CHUNKS : (c + 1) * CHUNKS, :] = from_table(table[c * SLOTS : (c + 1) * SLOTS])
    for i in range(CHUNKS):
        ref[:, i * LANES : (i + 1) * LANES] = stage[pl.ds(i, 3, stride=CHUNKS), :]


def gather(table_parts, hot, rows):
    picked = dot(table_parts, hot)
    total = picked[:rows]
    for k in range(1, table_parts.shape[0] // rows):
        total = total + picked[k * rows : (k + 1) * rows]
    return total


def send_pieces(table, rows, send_ref, first_ref, second_ref):
    parts = jnp.concatenate(split(table[:rows], 3), axis=0)
    half = CLUSTERS // 2
    for k, out in enumerate((first_ref, second_ref)):
        hot = one_hot(cluster_column(send_ref[:, k * half : (k + 1) * half]), CLUSTERS)
        out[...] = gather(parts, hot, rows)


def prepare(
    positions_far, radius_far, mask_far, send_far, table_out, state_out, first, second,
    positions, radius, mask, send, stage, arrived,
):
    fetch(
        ((positions_far, positions), (radius_far, radius), (mask_far, mask), (send_far, send)), arrived
    )
    parts = load_components(positions, stage)
    reach = to_table(radius[...])
    weights = to_table(mask[...].astype(f32))
    real = weights > 0.5
    table = jnp.concatenate([jnp.where(real, part, FAR) for part in parts] + [reach], axis=0)
    table_out[...] = table
    for c in range(3):
        state_out[c * SLOTS : (c + 1) * SLOTS] = parts[c]
    state_out[3 * SLOTS :] = weights
    send_pieces(table, 4 * SLOTS, send, first, second)


def contacts(leading, partner, on_leading, on_partner, begin, end):
    step = 4

    def row(component, slot):
        return pl.ds(pl.multiple_of((component * SLOTS + slot) * 8, 8), 8)

    def some_slots(block, carry):
        base = block * step
        ours = [[leading[row(c, base + i), :] for c in range(4)] for i in range(step)]
        sums = [[jnp.zeros((8, LANES), f32) for _ in range(3)] for _ in range(step)]
        for q in range(SLOTS):
            theirs = [partner[row(c, q), :] for c in range(4)]
            back = [on_partner[row(c, q), :] for c in range(3)]
            for i in range(step):
                apart = [ours[i][c] - theirs[c] for c in range(3)]
                squared = apart[0] * apart[0] + apart[1] * apart[1] + apart[2] * apart[2]
                reach = ours[i][3] + theirs[3]
                weight = jnp.maximum(reach * reach - squared, 0.0)
                for c in range(3):
                    push = weight * apart[c]
                    sums[i][c] = sums[i][c] + push
                    back[c] = back[c] + push
            for c in range(3):
                on_partner[row(c, q), :] = back[c]
        for i in range(step):
            for c in range(3):
                on_leading[row(c, base + i), :] = sums[i][c]
        return carry

    lax.fori_loop(begin // step, end // step, some_slots, 0)


def fill_hot(pairs, row, column, hot):
    width = 2 * LANES
    for block in range(PAIRS // width):
        span = slice(block * width, (block + 1) * width)
        hot[:, span] = one_hot(column(pairs[row : row + 1, span]), CLUSTERS)


def fill_slots(parts, hot, pairs, landed):
    width = 2 * LANES
    for block in range(PAIRS // width):
        span = slice(block * width, (block + 1) * width)
        picked = gather(parts, hot[:, span], 4 * SLOTS)
        if pairs is not None:
            offsets = pairs[2:5, span].astype(f32)
            picked = jnp.concatenate(
                [picked[c * SLOTS : (c + 1) * SLOTS] - offsets[c : c + 1] for c in range(3)]
                + [picked[3 * SLOTS :]],
                axis=0,
            )
        for k in range(2):
            landed[pl.ds(2 * block + k, 4 * SLOTS, stride=8), :] = picked[
                :, k * LANES : (k + 1) * LANES
            ]


def scatter(sums, hot):
    pieces = jnp.concatenate(
        [sums[pl.ds(k, 3 * SLOTS, stride=8), :] for k in range(PAIRS // LANES)], axis=1
    )
    added = dot_lanes(jnp.concatenate(split(pieces, 2), axis=0), hot[...])
    return added[: 3 * SLOTS] + added[3 * SLOTS :]


def table_parts(table):
    return jnp.concatenate(split(table[...], 3), axis=0)


INNER_SPLIT = 16


def inner_start(table, pairs, hot_a, hot_b, leading, partner, on_leading, on_partner):
    fill_hot(pairs, 0, cluster_column, hot_a)
    fill_hot(pairs, 1, cluster_column, hot_b)
    inner_again(table, pairs, hot_a, hot_b, leading, partner, on_leading, on_partner)


def inner_again(table, pairs, hot_a, hot_b, leading, partner, on_leading, on_partner):
    parts = table_parts(table)
    fill_slots(parts, hot_a, pairs, leading)
    fill_slots(parts, hot_b, None, partner)
    on_partner[...] = jnp.zeros_like(on_partner)
    contacts(leading, partner, on_leading, on_partner, 0, INNER_SPLIT)


def inner_end(
    hot_a, hot_b, leading, partner, on_leading_first, on_partner_first, force, on_leading, on_partner
):
    for c in range(3):
        done = slice(c * SLOTS * 8, (c * SLOTS + INNER_SPLIT) * 8)
        on_leading[done, :] = on_leading_first[done, :]
    on_partner[...] = on_partner_first[...]
    contacts(leading, partner, on_leading, on_partner, INNER_SPLIT, SLOTS)
    force[...] = scatter(on_leading, hot_a) - scatter(on_partner, hot_b)


def cross_start(table, pairs, hot_a, hot_b, leading):
    fill_hot(pairs, 0, cluster_column, hot_a)
    fill_hot(pairs, 1, ghost_column, hot_b)
    cross_again(table, pairs, hot_a, leading)


def cross_again(table, pairs, hot_a, leading):
    fill_slots(table_parts(table), hot_a, pairs, leading)


def cross_end(on_leading, hot_a, force):
    force[...] = scatter(on_leading, hot_a)


def present_tile(low, high):
    here_x, here_y = lax.axis_index("gx"), lax.axis_index("gy")
    flags = []
    for slot in (low, high):
        a, b = NEIGHBOURS[slot]
        x, y = here_x + a, here_y + b
        inside = (x >= 0) & (x < lax.axis_size("gx")) & (y >= 0) & (y < lax.axis_size("gy"))
        flags.append(jnp.where(inside, 1, 0))
    return jnp.where(lower_half((1, LANES)), flags[0], flags[1]) > 0


def cross_kernel(
    leading, hot_b, reach, below, above, from_next, from_last,
    on_leading, up, down, keep, reach_out, partner, on_partner,
):
    rows = below.shape[0]
    low = lower_half((rows, LANES))
    tiles = [
        below[:, :LANES],
        jnp.where(low, above[:, LANES:], below[:, LANES:]),
        above[:, :LANES],
        jnp.where(low, from_last[:, LANES:], from_next[:, :LANES]),
    ]
    for k in range(4):
        there = present_tile(GHOST_ORDER[2 * k], GHOST_ORDER[2 * k + 1])
        placed = jnp.where(there, tiles[k][: 3 * SLOTS], FAR)
        size = reach[:, k * LANES : (k + 1) * LANES] if rows == 3 * SLOTS else tiles[k][3 * SLOTS :]
        reach_out[:, k * LANES : (k + 1) * LANES] = size
        tiles[k] = jnp.concatenate([placed, size], axis=0)
    ghosts = jnp.concatenate(tiles, axis=1)
    fill_slots(jnp.concatenate(split(ghosts, 3), axis=0), hot_b, None, partner)
    on_partner[...] = jnp.zeros_like(on_partner)
    contacts(leading, partner, on_leading, on_partner, 0, SLOTS)
    back = scatter(on_partner, hot_b)
    up[...] = back[:, : 2 * LANES]
    down[...] = back[:, LANES : 3 * LANES]
    keep[...] = back[:, 3 * LANES :]


def fetch(pairs, arrived):
    copies = [
        pltpu.make_async_copy(far, near, arrived.at[k]) for k, (far, near) in enumerate(pairs)
    ]
    for copy in copies:
        copy.start()
    for copy in copies:
        copy.wait()


def part_parcels(parcels, bit, stay, away):
    mine = (lax.axis_index("gy") & bit) > 0
    for k, low in enumerate([d for d in range(16) if not d & bit]):
        stay[k] = jnp.where(mine, parcels[low | bit], parcels[low])
        away[k] = jnp.where(mine, parcels[low], parcels[low | bit])


def join_parcels(stay, got, bit):
    mine = (lax.axis_index("gy") & bit) > 0
    parcels = [None] * 16
    for k, low in enumerate([d for d in range(16) if not d & bit]):
        parcels[low] = jnp.where(mine, got[k], stay[k])
        parcels[low | bit] = jnp.where(mine, stay[k], got[k])
    return parcels


def relay(bit):
    def relay_parcels(stay, got, stay_out, away_out):
        part_parcels(join_parcels(stay, got, bit), 2 * bit, stay_out, away_out)

    return relay_parcels


def deposit_kernel(
    velocity_far, radius_far, mask_far, cell_far, fluid_far, pressure_far,
    velocity_out, cell_out, totals_out, stay, away,
    velocity, radius, mask, cell, fluid, pressure, stage, arrived,
):
    fetch(
        (
            (velocity_far, velocity),
            (radius_far, radius),
            (mask_far, mask),
            (cell_far, cell),
            (fluid_far, fluid),
            (pressure_far, pressure),
        ),
        arrived,
    )
    parts = load_components(velocity, stage)
    reach = to_table(radius[...])
    weights = to_table(mask[...].astype(f32))
    cells = to_table(cell[...].astype(f32)).astype(jnp.int32)
    volumes = weights * ((4.0 * math.pi / 3.0) * reach * reach * reach)
    for c in range(3):
        velocity_out[c * SLOTS : (c + 1) * SLOTS] = parts[c]
    cell_out[...] = cells
    amounts = [volumes] + [volumes * part for part in parts]
    total = jnp.zeros((2 * 4 * 16, LANES), f32)
    for slot in range(SLOTS):
        cell_row = cells[slot : slot + 1]
        hot = one_hot(cell_row & (LANES - 1), LANES)
        group = lax.broadcasted_iota(jnp.int32, (16, CLUSTERS), 0) == (cell_row >> 7)
        spread = jnp.concatenate(
            [jnp.where(group, amount[slot : slot + 1], 0.0) for amount in amounts], axis=0
        )
        total = total + dot_lanes(jnp.concatenate(split(spread, 2), axis=0), hot)
    total = total[:64] + total[64:]
    totals_out[...] = total
    parcels = []
    for owner in range(16):
        span = slice(owner * LANES, (owner + 1) * LANES)
        parcels.append(
            jnp.concatenate(
                [total[c * 16 + owner : c * 16 + owner + 1] for c in range(4)]
                + [fluid[:, span] + time_step * pressure[:, span], jnp.zeros((1, LANES), f32)],
                axis=0,
            )
        )
    part_parcels(parcels, 1, stay, away)


def fluid_kernel(totals, stay, got, cell, at_grain, parcels_out):
    parcels = join_parcels(stay, got, 8)
    for source in range(16):
        parcels_out[source] = parcels[source]
    volume = totals[:16]
    void_here = jnp.maximum(1.0 - volume / cell_volume, void_floor)
    drag_rate = drag_factor * (1.1 - void_here) / (void_here * void_here)
    below = void_here + time_step * drag_rate * volume / cell_volume
    fields = []
    for c in range(3):
        momentum = drag_rate * totals[(c + 1) * 16 : (c + 2) * 16] / cell_volume
        driven = jnp.concatenate([parcels[k][4 + c : 5 + c] for k in range(16)], axis=0)
        fields.append((void_here * driven + time_step * momentum) / below)
    fields.append(drag_rate)
    parts = jnp.concatenate(split(jnp.concatenate(fields, axis=0), 2), axis=1)
    for slot in range(SLOTS):
        cell_row = cell[slot : slot + 1, :]
        hot = one_hot(cell_row & (LANES - 1), LANES)
        seen = dot(parts, jnp.concatenate([hot, hot], axis=0))
        group = lax.broadcasted_iota(jnp.int32, (16, CLUSTERS), 0) == (cell_row >> 7)
        for c in range(4):
            chosen = jnp.where(group, seen[c * 16 : (c + 1) * 16], 0.0)
            row = c * SLOTS + slot
            at_grain[row : row + 1, :] = jnp.sum(chosen, axis=0, keepdims=True)


def owned_kernel(parcels, fluid, pressure, fluid_out, void_out):
    for source in range(16):
        span = slice(source * LANES, (source + 1) * LANES)
        volume = parcels[source, 0:1, :]
        void_here = jnp.maximum(1.0 - volume / cell_volume, void_floor)
        drag_rate = drag_factor * (1.1 - void_here) / (void_here * void_here)
        below = void_here + time_step * drag_rate * volume / cell_volume
        push = void_here * pressure[:, span] + drag_rate * parcels[source, 1:4, :] / cell_volume
        fluid_out[:, span] = (void_here * fluid[:, span] + time_step * push) / below
        void_out[source : source + 1, :] = void_here


def advance(state, velocity, reach, at_grain, inner, cross, above, below, from_last, from_next, send):
    low = lower_half((3 * SLOTS, LANES))
    tiles = [
        from_last[:, :LANES],
        jnp.where(low, from_last[:, LANES:], below[:, LANES:]),
        jnp.where(low, above[:, :LANES], from_next[:, :LANES]),
        from_next[:, LANES:],
    ]
    tiles = [jnp.where(present_tile(2 * k, 2 * k + 1), tiles[k], 0.0) for k in range(4)]
    returned = jnp.concatenate(tiles, axis=1)
    hot = one_hot(cluster_column(send[...]), CLUSTERS)
    added = dot_lanes(jnp.concatenate(split(returned, 2), axis=0), hot)
    contact = spring * (inner[...] + cross[...] - (added[: 3 * SLOTS] + added[3 * SLOTS :]))
    weights = state[3 * SLOTS :, :]
    sphere = (4.0 * math.pi / 3.0) * reach * reach * reach
    masses = grain_density * sphere
    volumes = weights * sphere
    drag = at_grain[3 * SLOTS :, :] * volumes
    places, speeds = [], []
    for c in range(3):
        rows = slice(c * SLOTS, (c + 1) * SLOTS)
        speed = velocity[rows, :]
        pull = (contact[rows] + drag * (at_grain[rows, :] - speed)) / masses
        if c == 2:
            pull = pull - gravity
        speed = speed + time_step * weights * pull
        speeds.append(speed)
        places.append(state[rows, :] + time_step * weights * speed)
    return places, speeds, weights


def middle_kernel(
    table, state, velocity, at_grain, inner, cross, above, below, from_last, from_next, send,
    table_out, state_out, velocity_out, first, second,
):
    reach = table[3 * SLOTS :, :]
    places, speeds, weights = advance(
        state, velocity, reach, at_grain, inner, cross, above, below, from_last, from_next, send
    )
    real = weights > 0.5
    moved = jnp.concatenate([jnp.where(real, place, FAR) for place in places] + [reach], axis=0)
    table_out[...] = moved
    for c in range(3):
        state_out[c * SLOTS : (c + 1) * SLOTS] = places[c]
        velocity_out[c * SLOTS : (c + 1) * SLOTS] = speeds[c]
    state_out[3 * SLOTS :] = weights
    send_pieces(moved, 3 * SLOTS, send, first, second)


def last_kernel(
    table, state, velocity, at_grain, inner, cross, above, below, from_last, from_next, send,
    positions_out, velocity_out, stage,
):
    places, speeds, _ = advance(
        state, velocity, table[3 * SLOTS :, :], at_grain, inner, cross, above, below, from_last,
        from_next, send,
    )
    store_components(positions_out, stage, jnp.concatenate(places, axis=0))
    store_components(velocity_out, stage, jnp.concatenate(speeds, axis=0))


def shift(array, step_x, step_y):
    size_x, size_y = lax.axis_size("gx"), lax.axis_size("gy")
    moves = []
    for x in range(size_x):
        for y in range(size_y):
            target = (x + step_x) % size_x * size_y + (y + step_y) % size_y
            moves.append((x * size_y + y, target))
    return lax.ppermute(array, ("gx", "gy"), moves)


def swap(array, bit):
    size_x, size_y = lax.axis_size("gx"), lax.axis_size("gy")
    moves = [(x * size_y + y, x * size_y + (y ^ bit)) for x in range(size_x) for y in range(size_y)]
    return lax.ppermute(array, ("gx", "gy"), moves)


def halves(low_from, high_from):
    return jnp.where(lower_half(low_from.shape), low_from, high_from)


def pass_ghosts(first, second, from_next, from_last):
    minus = jnp.concatenate(
        [halves(from_next[:, :LANES], from_last[:, :LANES]), first[:, LANES:]], axis=1
    )
    plus = jnp.concatenate(
        [halves(from_next[:, LANES:], from_last[:, LANES:]), second[:, :LANES]], axis=1
    )
    return minus, plus


def pass_forces(above, below, keep):
    first = jnp.concatenate([halves(below[:, :LANES], keep), above[:, LANES:]], axis=1)
    second = jnp.concatenate([below[:, :LANES], halves(keep, above[:, LANES:])], axis=1)
    return first, second


def table_shape(rows, columns=CLUSTERS):
    return jax.ShapeDtypeStruct((rows, columns), f32)


STAGE = pltpu.VMEM((3 * CHUNKS, LANES), f32)
HOT = jax.ShapeDtypeStruct((CLUSTERS, PAIRS), bf16)
SLOT_ROWS = table_shape(4 * SLOTS * 8, LANES)
FORCE_ROWS = table_shape(3 * SLOTS * 8, LANES)
FORCE_SCRATCH = pltpu.VMEM((3 * SLOTS * 8, LANES), f32)
PARCELS = jax.ShapeDtypeStruct((8, 8, LANES), f32)


def call(kernel, out_shape, operands, scratch=(), cost=1.0, far=False, after=()):
    count = len(operands)

    def body(*refs):
        kernel(*refs[:count], *refs[count + len(after) :])

    space = pltpu.HBM if far else pltpu.VMEM
    if far:
        operands = tuple(pltpu.with_memory_space_constraint(array, pltpu.HBM) for array in operands)
    return pl.pallas_call(
        body,
        out_shape=out_shape,
        in_specs=[pl.BlockSpec(memory_space=space)] * count
        + [pl.BlockSpec(memory_space=pl.ANY)] * len(after),
        scratch_shapes=list(scratch),
        compiler_params=PARAMS,
        cost_estimate=pl.CostEstimate(
            flops=int(cost * 10**9), bytes_accessed=int(cost * 10**6), transcendentals=0
        ),
        name=kernel.__name__,
    )(*operands, *after)


def shards(
    positions,
    velocity,
    radius,
    grain_mask,
    grain_cell,
    inner_pairs,
    cross_pairs,
    send_lists,
    fluid_velocity,
    pressure_grad,
):
    send = send_lists.reshape(1, -1)
    radius = radius.reshape(CHUNKS, LANES)
    mask = grain_mask.reshape(CHUNKS, LANES)
    cell = grain_cell.reshape(CHUNKS, LANES)

    full, wide = table_shape(4 * SLOTS), table_shape(4 * SLOTS, 2 * LANES)
    narrow, single = table_shape(3 * SLOTS, 2 * LANES), table_shape(3 * SLOTS, LANES)
    three, reach = table_shape(3 * SLOTS), table_shape(SLOTS)

    def near(array):
        return pltpu.VMEM(array.shape, array.dtype)

    operands = (positions, radius, mask, send)
    table, state, first, second = call(
        prepare,
        (full, full, wide, wide),
        operands,
        [near(array) for array in operands] + [STAGE, pltpu.SemaphoreType.DMA((4,))],
        far=True,
    )
    operands = (velocity, radius, mask, cell, fluid_velocity, pressure_grad)
    moving, cells, totals, stay, away = call(
        deposit_kernel,
        (
            three,
            jax.ShapeDtypeStruct((SLOTS, CLUSTERS), jnp.int32),
            table_shape(64, LANES),
            PARCELS,
            PARCELS,
        ),
        operands,
        [near(array) for array in operands] + [STAGE, pltpu.SemaphoreType.DMA((6,))],
        3,
        far=True,
        after=(table,),
    )
    got = swap(away, 1)

    ghost_reach = jnp.zeros((SLOTS, CLUSTERS), f32)
    for substep in range(2):
        from_next, from_last = shift(first, -1, 0), shift(second, 1, 0)
        minus, plus = pass_ghosts(first, second, from_next, from_last)
        below, above = shift(minus, 0, -1), shift(plus, 0, 1)
        if substep == 0:
            hot_a, hot_b, *rows = call(
                inner_start,
                (HOT, HOT, SLOT_ROWS, SLOT_ROWS, FORCE_ROWS, FORCE_ROWS),
                (table, inner_pairs),
                cost=3,
                after=(minus, plus),
            )
            stay, away = call(relay(1), (PARCELS, PARCELS), (stay, got), after=(rows[0],))
            got = swap(away, 2)
            hot_c, hot_d, leading = call(
                cross_start, (HOT, HOT, SLOT_ROWS), (table, cross_pairs), after=(away,)
            )
        else:
            rows = call(
                inner_again,
                (SLOT_ROWS, SLOT_ROWS, FORCE_ROWS, FORCE_ROWS),
                (table, inner_pairs, hot_a, hot_b),
                cost=3,
            )
            leading = call(
                cross_again, SLOT_ROWS, (table, cross_pairs, hot_c), after=(minus, plus, rows[0])
            )
        on_leading, up, down, keep, ghost_reach = call(
            cross_kernel,
            (FORCE_ROWS, narrow, narrow, single, reach),
            (leading, hot_d, ghost_reach, below, above, from_next, from_last),
            [pltpu.VMEM(SLOT_ROWS.shape, f32), FORCE_SCRATCH],
            4,
        )
        below, above = shift(up, 0, 1), shift(down, 0, -1)
        if substep == 0:
            stay, away = call(relay(2), (PARCELS, PARCELS), (stay, got), after=(keep,))
            got = swap(away, 4)
        inner = call(
            inner_end,
            three,
            (hot_a, hot_b, *rows),
            [FORCE_SCRATCH, FORCE_SCRATCH],
            3,
            after=(keep, away),
        )
        cross = call(cross_end, three, (on_leading, hot_c), after=(away,))
        if substep == 0:
            stay, away = call(relay(4), (PARCELS, PARCELS), (stay, got), after=(inner, cross))
            got = swap(away, 8)
        first, second = pass_forces(above, below, keep)
        from_last, from_next = shift(first, 1, 0), shift(second, -1, 0)
        if substep == 0:
            at_grain, parcels = call(
                fluid_kernel,
                (full, jax.ShapeDtypeStruct((16, 8, LANES), f32)),
                (totals, stay, got, cells),
                (),
                3,
                after=(first, second),
            )
        else:
            fluid_out, void_out = call(
                owned_kernel,
                (jax.ShapeDtypeStruct(fluid_velocity.shape, f32), table_shape(16, LANES)),
                (parcels, fluid_velocity, pressure_grad),
                after=(first, second),
            )
        operands = (
            table, state, moving, at_grain, inner, cross, above, below, from_last, from_next, send
        )
        if substep == 0:
            table, state, moving, first, second = call(
                middle_kernel, (full, full, three, narrow, narrow), operands
            )
        else:
            shape = jax.ShapeDtypeStruct(positions.shape, f32)
            positions, velocity = call(last_kernel, (shape, shape), operands, [STAGE])
    return positions, velocity, fluid_out, void_out.reshape(-1)


def solution(mesh):
    placed = (
        P(None, ("gx", "gy")),
        P(None, ("gx", "gy")),
        P(("gx", "gy")),
        P(("gx", "gy")),
        P(("gx", "gy")),
        P(None, ("gx", "gy")),
        P(None, ("gx", "gy")),
        P(("gx", "gy")),
        P(None, ("gx", "gy")),
        P(None, ("gx", "gy")),
    )
    return jax.shard_map(
        shards,
        mesh=mesh,
        in_specs=placed,
        out_specs=(
            P(None, ("gx", "gy")),
            P(None, ("gx", "gy")),
            P(None, ("gx", "gy")),
            P(("gx", "gy")),
        ),
        check_vma=False,
    )
```

```python
import math

import jax
import jax.numpy as jnp
from jax import lax
from jax.experimental import pallas as pl
from jax.experimental.pallas import tpu as pltpu
from jax.sharding import PartitionSpec as P

SLOTS = 32
LANES = 128
CLUSTERS = 512
GHOSTS = 64
PAIRS = 1024
CHUNKS = 128
GROUP = 4
NEIGHBOURS = ((-1, -1), (-1, 0), (-1, 1), (0, -1), (0, 1), (1, -1), (1, 0), (1, 1))
GHOST_ORDER = (7, 2, 3, 4, 5, 0, 1, 6)
FAR = 2.0**30

spring = 4.0
time_step = 0.1
grain_density = 2.65
gravity = 1.0
cell_volume = 4.0
void_floor = 0.35
drag_factor = 0.5

f32 = jnp.float32
bf16 = jnp.bfloat16
PARAMS = pltpu.CompilerParams(vmem_limit_bytes=24 * 1024 * 1024)


def split(values, parts):
    pieces = []
    for _ in range(parts - 1):
        piece = values.astype(bf16)
        pieces.append(piece)
        values = values - piece.astype(f32)
    pieces.append(values.astype(bf16))
    return pieces


def one_hot(index_row, count):
    rows = lax.broadcasted_iota(jnp.int32, (count, index_row.shape[1]), 0)
    return jnp.where(rows == index_row, 1.0, 0.0).astype(bf16)


def dot(left, right):
    return jnp.dot(left, right, preferred_element_type=f32)


def dot_lanes(left, right):
    return lax.dot_general(left, right, (((1,), (1,)), ((), ())), preferred_element_type=f32)


def cluster_column(index):
    return (index & (GROUP - 1)) * LANES + (index >> 2)


def ghost_column(slot):
    block = slot >> 6
    column = jnp.zeros_like(slot)
    for position, offset in enumerate(GHOST_ORDER):
        column = jnp.where(block == offset, position * GHOSTS, column)
    return column + (slot & (GHOSTS - 1))


def lower_half(shape):
    return lax.broadcasted_iota(jnp.int32, shape, 1) < GHOSTS


def by_parity(axis, even_first, even_second):
    even = lax.axis_index(axis) % 2 == 0
    return (
        jnp.where(even, even_first, even_second),
        jnp.where(even, even_second, even_first),
    )


def to_table(square):
    turned = square.T
    return jnp.concatenate([turned[k * SLOTS : (k + 1) * SLOTS] for k in range(GROUP)], axis=1)


def from_table(table):
    stacked = jnp.concatenate([table[:, k * LANES : (k + 1) * LANES] for k in range(GROUP)], axis=0)
    return stacked.T


def load_components(ref, stage):
    for i in range(CHUNKS):
        stage[pl.ds(i, 3, stride=CHUNKS), :] = ref[:, i * LANES : (i + 1) * LANES]
    return [to_table(stage[c * CHUNKS : (c + 1) * CHUNKS, :]) for c in range(3)]


def store_components(ref, stage, table):
    for c in range(3):
        stage[c * CHUNKS : (c + 1) * CHUNKS, :] = from_table(table[c * SLOTS : (c + 1) * SLOTS])
    for i in range(CHUNKS):
        ref[:, i * LANES : (i + 1) * LANES] = stage[pl.ds(i, 3, stride=CHUNKS), :]


def gather(table_parts, hot, rows):
    picked = dot(table_parts, hot)
    total = picked[:rows]
    for k in range(1, table_parts.shape[0] // rows):
        total = total + picked[k * rows : (k + 1) * rows]
    return total


def send_pieces(table, rows, hot, lead, trail):
    pieces = gather(jnp.concatenate(split(table[:rows], 3), axis=0), hot[...], rows)
    half = CLUSTERS // 2
    lead[...], trail[...] = by_parity("gy", pieces[:, half:], pieces[:, :half])


def prepare(
    positions_far, radius_far, mask_far, send_far, table_out, state_out, hot, lead, trail,
    positions, radius, mask, send, stage, arrived,
):
    fetch(
        ((positions_far, positions), (radius_far, radius), (mask_far, mask), (send_far, send)), arrived
    )
    parts = load_components(positions, stage)
    reach = to_table(radius[...])
    weights = to_table(mask[...].astype(f32))
    real = weights > 0.5
    table = jnp.concatenate([jnp.where(real, part, FAR) for part in parts] + [reach], axis=0)
    table_out[...] = table
    for c in range(3):
        state_out[c * SLOTS : (c + 1) * SLOTS] = parts[c]
    state_out[3 * SLOTS :] = weights
    hot[...] = one_hot(cluster_column(send[...]), CLUSTERS)
    send_pieces(table, 4 * SLOTS, hot, lead, trail)


def contacts(leading, partner, on_leading, on_partner, begin, end):
    step = 4

    def row(component, slot):
        return pl.ds(pl.multiple_of((component * SLOTS + slot) * 8, 8), 8)

    def some_slots(block, carry):
        base = block * step
        ours = [[leading[row(c, base + i), :] for c in range(4)] for i in range(step)]
        sums = [[jnp.zeros((8, LANES), f32) for _ in range(3)] for _ in range(step)]
        for q in range(SLOTS):
            theirs = [partner[row(c, q), :] for c in range(4)]
            back = [on_partner[row(c, q), :] for c in range(3)]
            for i in range(step):
                apart = [ours[i][c] - theirs[c] for c in range(3)]
                squared = apart[0] * apart[0] + apart[1] * apart[1] + apart[2] * apart[2]
                reach = ours[i][3] + theirs[3]
                weight = jnp.maximum(reach * reach - squared, 0.0)
                for c in range(3):
                    push = weight * apart[c]
                    sums[i][c] = sums[i][c] + push
                    back[c] = back[c] + push
            for c in range(3):
                on_partner[row(c, q), :] = back[c]
        for i in range(step):
            for c in range(3):
                on_leading[row(c, base + i), :] = sums[i][c]
        return carry

    lax.fori_loop(begin // step, end // step, some_slots, 0)


def fill_hot(pairs, row, column, hot):
    width = 2 * LANES
    for block in range(PAIRS // width):
        span = slice(block * width, (block + 1) * width)
        hot[:, span] = one_hot(column(pairs[row : row + 1, span]), CLUSTERS)


def fill_slots(parts, hot, pairs, landed):
    width = 2 * LANES
    for block in range(PAIRS // width):
        span = slice(block * width, (block + 1) * width)
        picked = gather(parts, hot[:, span], 4 * SLOTS)
        if pairs is not None:
            offsets = pairs[2:5, span].astype(f32)
            picked = jnp.concatenate(
                [picked[c * SLOTS : (c + 1) * SLOTS] - offsets[c : c + 1] for c in range(3)]
                + [picked[3 * SLOTS :]],
                axis=0,
            )
        for k in range(2):
            landed[pl.ds(2 * block + k, 4 * SLOTS, stride=8), :] = picked[
                :, k * LANES : (k + 1) * LANES
            ]


def scatter(sums, hot):
    pieces = jnp.concatenate(
        [sums[pl.ds(k, 3 * SLOTS, stride=8), :] for k in range(PAIRS // LANES)], axis=1
    )
    added = dot_lanes(jnp.concatenate(split(pieces, 2), axis=0), hot[...])
    return added[: 3 * SLOTS] + added[3 * SLOTS :]


def table_parts(table):
    return jnp.concatenate(split(table[...], 3), axis=0)


INNER_SPLIT = 16


def inner_start(table, pairs, hot_a, hot_b, leading, partner, on_leading, on_partner):
    fill_hot(pairs, 0, cluster_column, hot_a)
    fill_hot(pairs, 1, cluster_column, hot_b)
    inner_again(table, pairs, hot_a, hot_b, leading, partner, on_leading, on_partner)


def inner_again(table, pairs, hot_a, hot_b, leading, partner, on_leading, on_partner):
    parts = table_parts(table)
    fill_slots(parts, hot_a, pairs, leading)
    fill_slots(parts, hot_b, None, partner)
    on_partner[...] = jnp.zeros_like(on_partner)
    contacts(leading, partner, on_leading, on_partner, 0, INNER_SPLIT)
    for c in range(3):
        later = slice((c * SLOTS + INNER_SPLIT) * 8, (c + 1) * SLOTS * 8)
        on_leading[later, :] = jnp.zeros(((SLOTS - INNER_SPLIT) * 8, LANES), f32)


def inner_rest(leading, partner, on_leading_first, on_partner_first, on_leading, on_partner):
    for c in range(3):
        done = slice(c * SLOTS * 8, (c * SLOTS + INNER_SPLIT) * 8)
        on_leading[done, :] = on_leading_first[done, :]
    on_partner[...] = on_partner_first[...]
    contacts(leading, partner, on_leading, on_partner, INNER_SPLIT, SLOTS)


def cross_start(table, pairs, hot_a, hot_b, leading):
    fill_hot(pairs, 0, cluster_column, hot_a)
    fill_hot(pairs, 1, ghost_column, hot_b)
    cross_again(table, pairs, hot_a, leading)


def cross_again(table, pairs, hot_a, leading):
    fill_slots(table_parts(table), hot_a, pairs, leading)


def scatter_kernel(on_leading, on_partner, on_crossing, hot_a, hot_b, hot_c, force):
    force[...] = (
        scatter(on_leading, hot_a) - scatter(on_partner, hot_b) + scatter(on_crossing, hot_c)
    )


def present_tile(low, high):
    here_x, here_y = lax.axis_index("gx"), lax.axis_index("gy")
    flags = []
    for slot in (low, high):
        a, b = NEIGHBOURS[slot]
        x, y = here_x + a, here_y + b
        inside = (x >= 0) & (x < lax.axis_size("gx")) & (y >= 0) & (y < lax.axis_size("gy"))
        flags.append(jnp.where(inside, 1, 0))
    return jnp.where(lower_half((1, LANES)), flags[0], flags[1]) > 0


def pass_ghosts(lead, trail, got_lead, got_trail, lead_out, trail_out, side):
    low = lower_half((lead.shape[0], LANES))
    own_second, own_first = by_parity("gy", lead[...], trail[...])
    from_last, from_next = by_parity("gy", got_lead[...], got_trail[...])
    minus = [jnp.where(low, from_next[:, :LANES], from_last[:, :LANES]), own_first[:, LANES:]]
    plus = [jnp.where(low, from_next[:, LANES:], from_last[:, LANES:]), own_second[:, :LANES]]
    for k in range(2):
        span = slice(k * LANES, (k + 1) * LANES)
        lead_out[:, span], trail_out[:, span] = by_parity("gx", plus[k], minus[k])
    side[...] = jnp.where(low, from_last[:, LANES:], from_next[:, :LANES])


def cross_contacts(ghosts, leading, hot_b, on_leading, lead, trail, side_out, partner, on_partner):
    fill_slots(jnp.concatenate(split(ghosts, 3), axis=0), hot_b, None, partner)
    on_partner[...] = jnp.zeros_like(on_partner)
    contacts(leading, partner, on_leading, on_partner, 0, SLOTS)
    back = scatter(on_partner, hot_b)
    lead[...], trail[...] = by_parity("gx", back[:, : 2 * LANES], back[:, LANES : 3 * LANES])
    side_out[...] = back[:, 3 * LANES :]


def ghost_places(got_lead, got_trail, side):
    from_last, from_next = by_parity("gx", got_lead[...], got_trail[...])
    low = lower_half(side.shape)
    tiles = [
        from_next[:, :LANES],
        jnp.where(low, from_last[:, LANES:], from_next[:, LANES:]),
        from_last[:, :LANES],
        side[...],
    ]
    placed = [
        jnp.where(
            present_tile(GHOST_ORDER[2 * k], GHOST_ORDER[2 * k + 1]), tiles[k][: 3 * SLOTS], FAR
        )
        for k in range(4)
    ]
    return tiles, jnp.concatenate(placed, axis=1)


def cross_kernel(
    leading, hot_b, got_lead, got_trail, side,
    on_leading, lead, trail, side_out, reach_out, partner, on_partner,
):
    tiles, placed = ghost_places(got_lead, got_trail, side)
    reach = jnp.concatenate([tile[3 * SLOTS :] for tile in tiles], axis=1)
    reach_out[...] = reach
    ghosts = jnp.concatenate([placed, reach], axis=0)
    cross_contacts(ghosts, leading, hot_b, on_leading, lead, trail, side_out, partner, on_partner)


def cross_kernel_again(
    leading, hot_b, got_lead, got_trail, side, reach,
    on_leading, lead, trail, side_out, partner, on_partner,
):
    _, placed = ghost_places(got_lead, got_trail, side)
    ghosts = jnp.concatenate([placed, reach[...]], axis=0)
    cross_contacts(ghosts, leading, hot_b, on_leading, lead, trail, side_out, partner, on_partner)


def pass_forces(got_lead, got_trail, side, lead_out, trail_out, middle):
    low = lower_half((3 * SLOTS, LANES))
    from_last, from_next = by_parity("gx", got_lead[...], got_trail[...])
    up = [jnp.where(low, from_last[:, :LANES], side[...]), from_next[:, LANES:]]
    down = [from_last[:, :LANES], jnp.where(low, side[...], from_next[:, LANES:])]
    for k in range(2):
        span = slice(k * LANES, (k + 1) * LANES)
        lead_out[:, span], trail_out[:, span] = by_parity("gy", up[k], down[k])
    middle[...] = jnp.where(low, from_next[:, :LANES], from_last[:, LANES:])


def fetch(pairs, arrived):
    copies = [
        pltpu.make_async_copy(far, near, arrived.at[k]) for k, (far, near) in enumerate(pairs)
    ]
    for copy in copies:
        copy.start()
    for copy in copies:
        copy.wait()


def part_parcels(parcels, bit, stay, away):
    mine = (lax.axis_index("gy") & bit) > 0
    for k, low in enumerate([d for d in range(16) if not d & bit]):
        stay[k] = jnp.where(mine, parcels[low | bit], parcels[low])
        away[k] = jnp.where(mine, parcels[low], parcels[low | bit])


def join_parcels(stay, got, bit):
    mine = (lax.axis_index("gy") & bit) > 0
    parcels = [None] * 16
    for k, low in enumerate([d for d in range(16) if not d & bit]):
        parcels[low] = jnp.where(mine, got[k], stay[k])
        parcels[low | bit] = jnp.where(mine, stay[k], got[k])
    return parcels


def relay(bit):
    def relay_parcels(stay, got, stay_out, away_out):
        part_parcels(join_parcels(stay, got, bit), 2 * bit, stay_out, away_out)

    return relay_parcels


def deposit_kernel(
    velocity_far, radius_far, mask_far, cell_far, fluid_far, pressure_far, inner_far, cross_far,
    velocity_out, cell_out, totals_out, stay, away, fluid, pressure, inner, cross,
    velocity, radius, mask, cell, stage, arrived,
):
    fetch(
        (
            (velocity_far, velocity),
            (radius_far, radius),
            (mask_far, mask),
            (cell_far, cell),
            (fluid_far, fluid),
            (pressure_far, pressure),
            (inner_far, inner),
            (cross_far, cross),
        ),
        arrived,
    )
    parts = load_components(velocity, stage)
    reach = to_table(radius[...])
    weights = to_table(mask[...].astype(f32))
    cells = to_table(cell[...].astype(f32)).astype(jnp.int32)
    volumes = weights * ((4.0 * math.pi / 3.0) * reach * reach * reach)
    for c in range(3):
        velocity_out[c * SLOTS : (c + 1) * SLOTS] = parts[c]
    cell_out[...] = cells
    amounts = [volumes] + [volumes * part for part in parts]
    total = jnp.zeros((2 * 4 * 16, LANES), f32)
    for slot in range(SLOTS):
        cell_row = cells[slot : slot + 1]
        hot = one_hot(cell_row & (LANES - 1), LANES)
        group = lax.broadcasted_iota(jnp.int32, (16, CLUSTERS), 0) == (cell_row >> 7)
        spread = jnp.concatenate(
            [jnp.where(group, amount[slot : slot + 1], 0.0) for amount in amounts], axis=0
        )
        total = total + dot_lanes(jnp.concatenate(split(spread, 2), axis=0), hot)
    total = total[:64] + total[64:]
    totals_out[...] = total
    parcels = []
    for owner in range(16):
        span = slice(owner * LANES, (owner + 1) * LANES)
        parcels.append(
            jnp.concatenate(
                [total[c * 16 + owner : c * 16 + owner + 1] for c in range(4)]
                + [fluid[:, span] + time_step * pressure[:, span], jnp.zeros((1, LANES), f32)],
                axis=0,
            )
        )
    part_parcels(parcels, 1, stay, away)


def fluid_kernel(totals, stay, got, cell, at_grain, parcels_out):
    parcels = join_parcels(stay, got, 8)
    for source in range(16):
        parcels_out[source] = parcels[source]
    volume = totals[:16]
    void_here = jnp.maximum(1.0 - volume / cell_volume, void_floor)
    drag_rate = drag_factor * (1.1 - void_here) / (void_here * void_here)
    below = void_here + time_step * drag_rate * volume / cell_volume
    fields = []
    for c in range(3):
        momentum = drag_rate * totals[(c + 1) * 16 : (c + 2) * 16] / cell_volume
        driven = jnp.concatenate([parcels[k][4 + c : 5 + c] for k in range(16)], axis=0)
        fields.append((void_here * driven + time_step * momentum) / below)
    fields.append(drag_rate)
    parts = jnp.concatenate(split(jnp.concatenate(fields, axis=0), 2), axis=1)
    for slot in range(SLOTS):
        cell_row = cell[slot : slot + 1, :]
        hot = one_hot(cell_row & (LANES - 1), LANES)
        seen = dot(parts, jnp.concatenate([hot, hot], axis=0))
        group = lax.broadcasted_iota(jnp.int32, (16, CLUSTERS), 0) == (cell_row >> 7)
        for c in range(4):
            chosen = jnp.where(group, seen[c * 16 : (c + 1) * 16], 0.0)
            row = c * SLOTS + slot
            at_grain[row : row + 1, :] = jnp.sum(chosen, axis=0, keepdims=True)


def owned_kernel(parcels, fluid, pressure, fluid_out, void_out):
    for source in range(16):
        span = slice(source * LANES, (source + 1) * LANES)
        volume = parcels[source, 0:1, :]
        void_here = jnp.maximum(1.0 - volume / cell_volume, void_floor)
        drag_rate = drag_factor * (1.1 - void_here) / (void_here * void_here)
        below = void_here + time_step * drag_rate * volume / cell_volume
        push = void_here * pressure[:, span] + drag_rate * parcels[source, 1:4, :] / cell_volume
        fluid_out[:, span] = (void_here * fluid[:, span] + time_step * push) / below
        void_out[source : source + 1, :] = void_here


def advance(state, velocity, reach, at_grain, force, middle, got_lead, got_trail, hot):
    low = lower_half((3 * SLOTS, LANES))
    from_last, from_next = by_parity("gy", got_lead[...], got_trail[...])
    tiles = [
        from_last[:, :LANES],
        jnp.where(low, from_last[:, LANES:], middle[...]),
        jnp.where(low, middle[...], from_next[:, :LANES]),
        from_next[:, LANES:],
    ]
    tiles = [jnp.where(present_tile(2 * k, 2 * k + 1), tiles[k], 0.0) for k in range(4)]
    returned = jnp.concatenate(tiles, axis=1)
    added = dot_lanes(jnp.concatenate(split(returned, 2), axis=0), hot[...])
    contact = spring * (force[...] - (added[: 3 * SLOTS] + added[3 * SLOTS :]))
    weights = state[3 * SLOTS :, :]
    sphere = (4.0 * math.pi / 3.0) * reach * reach * reach
    masses = grain_density * sphere
    volumes = weights * sphere
    drag = at_grain[3 * SLOTS :, :] * volumes
    places, speeds = [], []
    for c in range(3):
        rows = slice(c * SLOTS, (c + 1) * SLOTS)
        speed = velocity[rows, :]
        pull = (contact[rows] + drag * (at_grain[rows, :] - speed)) / masses
        if c == 2:
            pull = pull - gravity
        speed = speed + time_step * weights * pull
        speeds.append(speed)
        places.append(state[rows, :] + time_step * weights * speed)
    return places, speeds, weights


def middle_kernel(
    table, state, velocity, at_grain, force, middle, got_lead, got_trail, hot,
    table_out, state_out, velocity_out, lead, trail,
):
    reach = table[3 * SLOTS :, :]
    places, speeds, weights = advance(
        state, velocity, reach, at_grain, force, middle, got_lead, got_trail, hot
    )
    real = weights > 0.5
    moved = jnp.concatenate([jnp.where(real, place, FAR) for place in places] + [reach], axis=0)
    table_out[...] = moved
    for c in range(3):
        state_out[c * SLOTS : (c + 1) * SLOTS] = places[c]
        velocity_out[c * SLOTS : (c + 1) * SLOTS] = speeds[c]
    state_out[3 * SLOTS :] = weights
    send_pieces(moved, 3 * SLOTS, hot, lead, trail)


def last_kernel(
    table, state, velocity, at_grain, force, middle, got_lead, got_trail, hot,
    positions_out, velocity_out, stage,
):
    places, speeds, _ = advance(
        state, velocity, table[3 * SLOTS :, :], at_grain, force, middle, got_lead, got_trail, hot
    )
    store_components(positions_out, stage, jnp.concatenate(places, axis=0))
    store_components(velocity_out, stage, jnp.concatenate(speeds, axis=0))


def snake(array, axis, sign):
    size_x, size_y = lax.axis_size("gx"), lax.axis_size("gy")
    moves = []
    for x in range(size_x):
        for y in range(size_y):
            if axis == "gx":
                target = (x + (sign if y % 2 == 0 else -sign), y)
                target = target if 0 <= target[0] < size_x else (x, y ^ 1)
            else:
                target = (x, y + (sign if x % 2 == 0 else -sign))
                target = target if 0 <= target[1] < size_y else (x ^ 1, y)
            moves.append((x * size_y + y, target[0] * size_y + target[1]))
    return lax.ppermute(array, ("gx", "gy"), moves)


def swap(array, bit):
    size_x, size_y = lax.axis_size("gx"), lax.axis_size("gy")
    moves = [(x * size_y + y, x * size_y + (y ^ bit)) for x in range(size_x) for y in range(size_y)]
    return lax.ppermute(array, ("gx", "gy"), moves)


def table_shape(rows, columns=CLUSTERS):
    return jax.ShapeDtypeStruct((rows, columns), f32)


STAGE = pltpu.VMEM((3 * CHUNKS, LANES), f32)
HOT = jax.ShapeDtypeStruct((CLUSTERS, PAIRS), bf16)
SLOT_ROWS = table_shape(4 * SLOTS * 8, LANES)
FORCE_ROWS = table_shape(3 * SLOTS * 8, LANES)
FORCE_SCRATCH = pltpu.VMEM((3 * SLOTS * 8, LANES), f32)
PARCELS = jax.ShapeDtypeStruct((8, 8, LANES), f32)


def call(kernel, out_shape, operands, scratch=(), cost=1.0, far=False, after=()):
    count = len(operands)

    def body(*refs):
        kernel(*refs[:count], *refs[count + len(after) :])

    space = pltpu.HBM if far else pltpu.VMEM
    if far:
        operands = tuple(pltpu.with_memory_space_constraint(array, pltpu.HBM) for array in operands)
    return pl.pallas_call(
        body,
        out_shape=out_shape,
        in_specs=[pl.BlockSpec(memory_space=space)] * count
        + [pl.BlockSpec(memory_space=pl.ANY)] * len(after),
        scratch_shapes=list(scratch),
        compiler_params=PARAMS,
        cost_estimate=pl.CostEstimate(
            flops=int(cost * 10**9), bytes_accessed=int(cost * 10**6), transcendentals=0
        ),
        name=kernel.__name__,
    )(*operands, *after)


def shards(
    positions,
    velocity,
    radius,
    grain_mask,
    grain_cell,
    inner_pairs,
    cross_pairs,
    send_lists,
    fluid_velocity,
    pressure_grad,
):
    send = send_lists.reshape(1, -1)
    radius = radius.reshape(CHUNKS, LANES)
    mask = grain_mask.reshape(CHUNKS, LANES)
    cell = grain_cell.reshape(CHUNKS, LANES)

    full, wide = table_shape(4 * SLOTS), table_shape(4 * SLOTS, 2 * LANES)
    narrow, single = table_shape(3 * SLOTS, 2 * LANES), table_shape(3 * SLOTS, LANES)
    three, full_tile = table_shape(3 * SLOTS), table_shape(4 * SLOTS, LANES)

    def near(array):
        return pltpu.VMEM(array.shape, array.dtype)

    def like(array):
        return jax.ShapeDtypeStruct(array.shape, array.dtype)

    operands = (positions, radius, mask, send)
    table, state, hot, lead, trail = call(
        prepare,
        (full, full, jax.ShapeDtypeStruct((CLUSTERS, CLUSTERS), bf16), wide, wide),
        operands,
        [near(array) for array in operands] + [STAGE, pltpu.SemaphoreType.DMA((4,))],
        far=True,
    )
    operands = (velocity, radius, mask, cell, fluid_velocity, pressure_grad, inner_pairs, cross_pairs)
    moving, cells, totals, stay, away, fluid, pressure, inner_pairs, cross_pairs = call(
        deposit_kernel,
        (
            three,
            jax.ShapeDtypeStruct((SLOTS, CLUSTERS), jnp.int32),
            table_shape(64, LANES),
            PARCELS,
            PARCELS,
            *[like(array) for array in operands[4:]],
        ),
        operands,
        [near(array) for array in operands[:4]] + [STAGE, pltpu.SemaphoreType.DMA((8,))],
        3,
        far=True,
        after=(table,),
    )
    got = swap(away, 1)

    cross_scratch = [pltpu.VMEM(SLOT_ROWS.shape, f32), FORCE_SCRATCH]
    for substep in range(2):
        first = substep == 0
        got_lead, got_trail = snake(lead, "gx", 1), snake(trail, "gx", -1)
        if not first:
            rows = call(
                inner_again,
                (SLOT_ROWS, SLOT_ROWS, FORCE_ROWS, FORCE_ROWS),
                (table, inner_pairs, hot_a, hot_b),
                cost=3,
            )
        lead, trail, side = call(
            pass_ghosts,
            (wide, wide, full_tile) if first else (narrow, narrow, single),
            (lead, trail, got_lead, got_trail),
            after=(away,) if first else (rows[3],),
        )
        got_lead, got_trail = snake(lead, "gy", 1), snake(trail, "gy", -1)
        if first:
            stay, away = call(relay(1), (PARCELS, PARCELS), (stay, got), after=(lead, trail))
            got = swap(away, 2)
            hot_a, hot_b, *rows = call(
                inner_start,
                (HOT, HOT, SLOT_ROWS, SLOT_ROWS, FORCE_ROWS, FORCE_ROWS),
                (table, inner_pairs),
                cost=3,
                after=(away,),
            )
            hot_c, hot_d, leading = call(
                cross_start, (HOT, HOT, SLOT_ROWS), (table, cross_pairs), after=(rows[3],)
            )
            stay, away = call(relay(2), (PARCELS, PARCELS), (stay, got), after=(leading,))
            got = swap(away, 4)
            on_crossing, lead, trail, side, reach = call(
                cross_kernel,
                (FORCE_ROWS, narrow, narrow, single, table_shape(SLOTS)),
                (leading, hot_d, got_lead, got_trail, side),
                cross_scratch,
                4,
                after=(away,),
            )
        else:
            leading = call(
                cross_again, SLOT_ROWS, (table, cross_pairs, hot_c), after=(lead, trail)
            )
            sums = call(inner_rest, (FORCE_ROWS, FORCE_ROWS), rows, cost=2, after=(leading,))
            on_crossing, lead, trail, side = call(
                cross_kernel_again,
                (FORCE_ROWS, narrow, narrow, single),
                (leading, hot_d, got_lead, got_trail, side, reach),
                cross_scratch,
                4,
                after=(sums[1],),
            )
        got_lead, got_trail = snake(lead, "gy", 1), snake(trail, "gy", -1)
        if first:
            stay, away = call(relay(4), (PARCELS, PARCELS), (stay, got), after=(side,))
            got = swap(away, 8)
            sums = call(inner_rest, (FORCE_ROWS, FORCE_ROWS), rows, cost=2, after=(away,))
        force = call(
            scatter_kernel, three, (*sums, on_crossing, hot_a, hot_b, hot_c), cost=2, after=(side,)
        )
        lead, trail, middle = call(
            pass_forces, (narrow, narrow, single), (got_lead, got_trail, side), after=(force,)
        )
        got_lead, got_trail = snake(lead, "gx", 1), snake(trail, "gx", -1)
        if first:
            at_grain, parcels = call(
                fluid_kernel,
                (full, jax.ShapeDtypeStruct((16, 8, LANES), f32)),
                (totals, stay, got, cells),
                (),
                3,
                after=(lead, trail),
            )
        else:
            fluid_out, void_out = call(
                owned_kernel,
                (like(fluid_velocity), table_shape(16, LANES)),
                (parcels, fluid, pressure),
                after=(lead, trail),
            )
        operands = (table, state, moving, at_grain, force, middle, got_lead, got_trail, hot)
        if first:
            table, state, moving, lead, trail = call(
                middle_kernel, (full, full, three, narrow, narrow), operands
            )
        else:
            positions, velocity = call(
                last_kernel, (like(positions), like(positions)), operands, [STAGE]
            )
    return positions, velocity, fluid_out, void_out.reshape(-1)


def solution(mesh):
    placed = (
        P(None, ("gx", "gy")),
        P(None, ("gx", "gy")),
        P(("gx", "gy")),
        P(("gx", "gy")),
        P(("gx", "gy")),
        P(None, ("gx", "gy")),
        P(None, ("gx", "gy")),
        P(("gx", "gy")),
        P(None, ("gx", "gy")),
        P(None, ("gx", "gy")),
    )
    return jax.shard_map(
        shards,
        mesh=mesh,
        in_specs=placed,
        out_specs=(
            P(None, ("gx", "gy")),
            P(None, ("gx", "gy")),
            P(None, ("gx", "gy")),
            P(("gx", "gy")),
        ),
        check_vma=False,
    )
```

```python
import math

import jax
import jax.numpy as jnp
from jax import lax
from jax.experimental import pallas as pl
from jax.experimental.pallas import tpu as pltpu
from jax.sharding import PartitionSpec as P

SLOTS = 32
LANES = 128
CLUSTERS = 512
GHOSTS = 64
PAIRS = 1024
CHUNKS = 128
GROUP = 4
NEIGHBOURS = ((-1, -1), (-1, 0), (-1, 1), (0, -1), (0, 1), (1, -1), (1, 0), (1, 1))
GHOST_ORDER = (7, 2, 3, 4, 5, 0, 1, 6)
FAR = 2.0**30

spring = 4.0
time_step = 0.1
grain_density = 2.65
gravity = 1.0
cell_volume = 4.0
void_floor = 0.35
drag_factor = 0.5

f32 = jnp.float32
bf16 = jnp.bfloat16
PARAMS = pltpu.CompilerParams(vmem_limit_bytes=24 * 1024 * 1024)


def split(values, parts):
    pieces = []
    for _ in range(parts - 1):
        piece = values.astype(bf16)
        pieces.append(piece)
        values = values - piece.astype(f32)
    pieces.append(values.astype(bf16))
    return pieces


def one_hot(index_row, count):
    width = index_row.shape[1]
    rows = lax.broadcasted_iota(jnp.int32, (LANES, width), 0).astype(f32).astype(bf16)
    blocks = []
    for k in range(count // LANES):
        within = index_row - k * LANES
        within = jnp.where((within >= 0) & (within < LANES), within, -1).astype(f32).astype(bf16)
        blocks.append(jnp.where(rows == within, jnp.ones((), bf16), jnp.zeros((), bf16)))
    return jnp.concatenate(blocks, axis=0) if len(blocks) > 1 else blocks[0]


def dot(left, right):
    return jnp.dot(left, right, preferred_element_type=f32)


def dot_lanes(left, right):
    return lax.dot_general(left, right, (((1,), (1,)), ((), ())), preferred_element_type=f32)


def cluster_column(index):
    return (index & (GROUP - 1)) * LANES + (index >> 2)


def ghost_column(slot):
    block = slot >> 6
    column = jnp.zeros_like(slot)
    for position, offset in enumerate(GHOST_ORDER):
        column = jnp.where(block == offset, position * GHOSTS, column)
    return column + (slot & (GHOSTS - 1))


def lower_half(shape):
    return lax.broadcasted_iota(jnp.int32, shape, 1) < GHOSTS


def swap_halves(tile):
    return jnp.concatenate([tile[:, GHOSTS:], tile[:, :GHOSTS]], axis=1)


def fold(whole, half, upper):
    rows = half.shape[0] // 2
    low = lower_half((rows, LANES))
    if upper:
        packed = jnp.where(low, swap_halves(half[:rows]), half[rows:])
    else:
        packed = jnp.where(low, half[:rows], swap_halves(half[rows:]))
    return jnp.concatenate([whole, packed], axis=0)


def unfold(folded, upper):
    rows = folded.shape[0] // 3
    packed = folded[2 * rows :]
    turned = swap_halves(packed)
    half = [turned, packed] if upper else [packed, turned]
    return folded[: 2 * rows], jnp.concatenate(half, axis=0)


def by_parity(axis, even_first, even_second):
    even = lax.axis_index(axis) % 2 == 0
    return (
        jnp.where(even, even_first, even_second),
        jnp.where(even, even_second, even_first),
    )


def to_table(square):
    turned = square.T
    return jnp.concatenate([turned[k * SLOTS : (k + 1) * SLOTS] for k in range(GROUP)], axis=1)


def from_table(table):
    stacked = jnp.concatenate([table[:, k * LANES : (k + 1) * LANES] for k in range(GROUP)], axis=0)
    return stacked.T


def load_components(ref, stage):
    for i in range(CHUNKS):
        stage[pl.ds(i, 3, stride=CHUNKS), :] = ref[:, i * LANES : (i + 1) * LANES]
    return [to_table(stage[c * CHUNKS : (c + 1) * CHUNKS, :]) for c in range(3)]


def store_components(ref, stage, table):
    for c in range(3):
        stage[c * CHUNKS : (c + 1) * CHUNKS, :] = from_table(table[c * SLOTS : (c + 1) * SLOTS])
    for i in range(CHUNKS):
        ref[:, i * LANES : (i + 1) * LANES] = stage[pl.ds(i, 3, stride=CHUNKS), :]


def gather(table_parts, hot, rows):
    picked = dot(table_parts, hot)
    total = picked[:rows]
    for k in range(1, table_parts.shape[0] // rows):
        total = total + picked[k * rows : (k + 1) * rows]
    return total


def send_pieces(table, rows, hot, lead, trail, middle):
    pieces = gather(jnp.concatenate(split(table[:rows], 3), axis=0), hot[...], rows)
    tiles = [pieces[:, k * LANES : (k + 1) * LANES] for k in range(4)]
    up = fold(tiles[3], tiles[2], True)
    down = fold(tiles[0], tiles[1], False)
    lead[...], trail[...] = by_parity("gy", up, down)
    middle[...] = jnp.where(lower_half(tiles[1].shape), tiles[2], tiles[1])


def start_copies(pairs, arrived, first=0):
    copies = [
        pltpu.make_async_copy(far, near, arrived.at[first + k])
        for k, (far, near) in enumerate(pairs)
    ]
    for copy in copies:
        copy.start()
    return copies


def prepare(
    positions_far, radius_far, mask_far, send_far,
    velocity_far, cell_far, fluid_far, pressure_far, inner_far, cross_far,
    table_out, state_out, hot, lead, trail, middle, velocity, cell, fluid, pressure, inner, cross,
    positions, radius, mask, send, stage, arrived,
):
    needed = start_copies(
        ((positions_far, positions), (radius_far, radius), (mask_far, mask), (send_far, send)), arrived
    )
    later = start_copies(
        (
            (velocity_far, velocity),
            (cell_far, cell),
            (fluid_far, fluid),
            (pressure_far, pressure),
            (inner_far, inner),
            (cross_far, cross),
        ),
        arrived,
        4,
    )
    for copy in needed:
        copy.wait()
    parts = load_components(positions, stage)
    reach = to_table(radius[...])
    weights = to_table(mask[...].astype(f32))
    real = weights > 0.5
    table = jnp.concatenate([jnp.where(real, part, FAR) for part in parts] + [reach], axis=0)
    table_out[...] = table
    for c in range(3):
        state_out[c * SLOTS : (c + 1) * SLOTS] = parts[c]
    state_out[3 * SLOTS :] = weights
    hot[...] = one_hot(cluster_column(send[...]), CLUSTERS)
    send_pieces(table, 4 * SLOTS, hot, lead, trail, middle)
    for copy in later:
        copy.wait()


def contacts(leading, partner, on_leading, on_partner, begin, end):
    step = 4

    def row(component, slot):
        return pl.ds(pl.multiple_of((component * SLOTS + slot) * 8, 8), 8)

    def some_slots(block, carry):
        base = block * step
        ours = [[leading[row(c, base + i), :] for c in range(4)] for i in range(step)]
        sums = [[jnp.zeros((8, LANES), f32) for _ in range(3)] for _ in range(step)]
        for q in range(SLOTS):
            theirs = [partner[row(c, q), :] for c in range(4)]
            back = [on_partner[row(c, q), :] for c in range(3)]
            for i in range(step):
                apart = [ours[i][c] - theirs[c] for c in range(3)]
                squared = apart[0] * apart[0] + apart[1] * apart[1] + apart[2] * apart[2]
                reach = ours[i][3] + theirs[3]
                weight = jnp.maximum(reach * reach - squared, 0.0)
                for c in range(3):
                    push = weight * apart[c]
                    sums[i][c] = sums[i][c] + push
                    back[c] = back[c] + push
            for c in range(3):
                on_partner[row(c, q), :] = back[c]
        for i in range(step):
            for c in range(3):
                on_leading[row(c, base + i), :] = sums[i][c]
        return carry

    lax.fori_loop(begin // step, end // step, some_slots, 0)


def fill_hot(pairs, row, column, hot):
    width = 2 * LANES
    for block in range(PAIRS // width):
        span = slice(block * width, (block + 1) * width)
        hot[:, span] = one_hot(column(pairs[row : row + 1, span]), CLUSTERS)


def fill_slots(parts, hot, pairs, landed):
    width = 2 * LANES
    for block in range(PAIRS // width):
        span = slice(block * width, (block + 1) * width)
        picked = gather(parts, hot[:, span], 4 * SLOTS)
        if pairs is not None:
            offsets = pairs[2:5, span].astype(f32)
            picked = jnp.concatenate(
                [picked[c * SLOTS : (c + 1) * SLOTS] - offsets[c : c + 1] for c in range(3)]
                + [picked[3 * SLOTS :]],
                axis=0,
            )
        for k in range(2):
            landed[pl.ds(2 * block + k, 4 * SLOTS, stride=8), :] = picked[
                :, k * LANES : (k + 1) * LANES
            ]


def scatter(sums, hot):
    pieces = jnp.concatenate(
        [sums[pl.ds(k, 3 * SLOTS, stride=8), :] for k in range(PAIRS // LANES)], axis=1
    )
    added = dot_lanes(jnp.concatenate(split(pieces, 2), axis=0), hot[...])
    return added[: 3 * SLOTS] + added[3 * SLOTS :]


def table_parts(table):
    return jnp.concatenate(split(table[...], 2), axis=0)


INNER_SPLIT = 16


def inner_start(table, pairs, hot_a, hot_b, leading, partner, on_leading, on_partner):
    fill_hot(pairs, 0, cluster_column, hot_a)
    fill_hot(pairs, 1, cluster_column, hot_b)
    inner_again(table, pairs, hot_a, hot_b, leading, partner, on_leading, on_partner)


def inner_again(table, pairs, hot_a, hot_b, leading, partner, on_leading, on_partner):
    parts = table_parts(table)
    fill_slots(parts, hot_a, pairs, leading)
    fill_slots(parts, hot_b, None, partner)
    on_partner[...] = jnp.zeros_like(on_partner)
    contacts(leading, partner, on_leading, on_partner, 0, INNER_SPLIT)
    for c in range(3):
        later = slice((c * SLOTS + INNER_SPLIT) * 8, (c + 1) * SLOTS * 8)
        on_leading[later, :] = jnp.zeros(((SLOTS - INNER_SPLIT) * 8, LANES), f32)


def inner_rest(leading, partner, on_leading_first, on_partner_first, on_leading, on_partner):
    for c in range(3):
        done = slice(c * SLOTS * 8, (c * SLOTS + INNER_SPLIT) * 8)
        on_leading[done, :] = on_leading_first[done, :]
    on_partner[...] = on_partner_first[...]
    contacts(leading, partner, on_leading, on_partner, INNER_SPLIT, SLOTS)


def cross_start(table, pairs, hot_a, hot_b, leading):
    fill_hot(pairs, 0, cluster_column, hot_a)
    fill_hot(pairs, 1, ghost_column, hot_b)
    cross_again(table, pairs, hot_a, leading)


def cross_again(table, pairs, hot_a, leading):
    fill_slots(table_parts(table), hot_a, pairs, leading)


def scatter_kernel(on_leading, on_partner, on_crossing, hot_a, hot_b, hot_c, force):
    force[...] = (
        scatter(on_leading, hot_a) - scatter(on_partner, hot_b) + scatter(on_crossing, hot_c)
    )


def present_tile(low, high):
    here_x, here_y = lax.axis_index("gx"), lax.axis_index("gy")
    flags = []
    for slot in (low, high):
        a, b = NEIGHBOURS[slot]
        x, y = here_x + a, here_y + b
        inside = (x >= 0) & (x < lax.axis_size("gx")) & (y >= 0) & (y < lax.axis_size("gy"))
        flags.append(jnp.where(inside, 1, 0))
    return jnp.where(lower_half((1, LANES)), flags[0], flags[1]) > 0


def pass_ghosts(got_lead, got_trail, middle, lead_out, trail_out, side):
    low = lower_half(middle.shape)
    from_last, from_next = by_parity("gy", got_lead[...], got_trail[...])
    last_whole, last_half = unfold(from_last, True)
    next_whole, next_half = unfold(from_next, False)
    minus = fold(jnp.where(low, next_whole, last_half), middle[...], True)
    plus = fold(jnp.where(low, next_half, last_whole), middle[...], False)
    lead_out[...], trail_out[...] = by_parity("gx", plus, minus)
    side[...] = jnp.where(low, last_whole, next_whole)


def cross_contacts(ghosts, leading, hot_b, on_leading, lead, trail, side_out, partner, on_partner):
    fill_slots(table_parts(ghosts), hot_b, None, partner)
    on_partner[...] = jnp.zeros_like(on_partner)
    contacts(leading, partner, on_leading, on_partner, 0, SLOTS)
    back = scatter(on_partner, hot_b)
    tiles = [back[:, k * LANES : (k + 1) * LANES] for k in range(4)]
    up = fold(tiles[0], tiles[1], True)
    down = fold(tiles[2], tiles[1], False)
    lead[...], trail[...] = by_parity("gx", up, down)
    side_out[...] = tiles[3]


def ghost_places(got_lead, got_trail, side):
    from_last, from_next = by_parity("gx", got_lead[...], got_trail[...])
    last_whole, last_half = unfold(from_last, False)
    next_whole, next_half = unfold(from_next, True)
    low = lower_half(side.shape)
    tiles = [next_whole, jnp.where(low, last_half, next_half), last_whole, side[...]]
    placed = [
        jnp.where(
            present_tile(GHOST_ORDER[2 * k], GHOST_ORDER[2 * k + 1]), tiles[k][: 3 * SLOTS], FAR
        )
        for k in range(4)
    ]
    return tiles, jnp.concatenate(placed, axis=1)


def cross_kernel(
    leading, hot_b, got_lead, got_trail, side,
    on_leading, lead, trail, side_out, reach_out, partner, on_partner,
):
    tiles, placed = ghost_places(got_lead, got_trail, side)
    reach = jnp.concatenate([tile[3 * SLOTS :] for tile in tiles], axis=1)
    reach_out[...] = reach
    ghosts = jnp.concatenate([placed, reach], axis=0)
    cross_contacts(ghosts, leading, hot_b, on_leading, lead, trail, side_out, partner, on_partner)


def cross_kernel_again(
    leading, hot_b, got_lead, got_trail, side, reach,
    on_leading, lead, trail, side_out, partner, on_partner,
):
    _, placed = ghost_places(got_lead, got_trail, side)
    ghosts = jnp.concatenate([placed, reach[...]], axis=0)
    cross_contacts(ghosts, leading, hot_b, on_leading, lead, trail, side_out, partner, on_partner)


def pass_forces(got_lead, got_trail, side, lead_out, trail_out, middle):
    low = lower_half((3 * SLOTS, LANES))
    from_last, from_next = by_parity("gx", got_lead[...], got_trail[...])
    last_whole, last_half = unfold(from_last, True)
    next_whole, next_half = unfold(from_next, False)
    up = fold(jnp.where(low, last_whole, side[...]), next_whole, False)
    down = fold(jnp.where(low, side[...], next_whole), last_whole, True)
    lead_out[...], trail_out[...] = by_parity("gy", up, down)
    middle[...] = jnp.where(low, next_half, last_half)


def part_parcels(parcels, bit, stay, away):
    mine = (lax.axis_index("gy") & bit) > 0
    for k, low in enumerate([d for d in range(16) if not d & bit]):
        stay[k] = jnp.where(mine, parcels[low | bit], parcels[low])
        away[k] = jnp.where(mine, parcels[low], parcels[low | bit])


def join_parcels(stay, got, bit):
    mine = (lax.axis_index("gy") & bit) > 0
    parcels = [None] * 16
    for k, low in enumerate([d for d in range(16) if not d & bit]):
        parcels[low] = jnp.where(mine, got[k], stay[k])
        parcels[low | bit] = jnp.where(mine, stay[k], got[k])
    return parcels


def relay(bit):
    def relay_parcels(stay, got, stay_out, away_out):
        part_parcels(join_parcels(stay, got, bit), 2 * bit, stay_out, away_out)

    return relay_parcels


def deposit_kernel(
    table, state, velocity, cell, fluid, pressure, velocity_out, cell_out, totals_out, stay, away, stage
):
    parts = load_components(velocity, stage)
    reach = table[3 * SLOTS :, :]
    weights = state[3 * SLOTS :, :]
    cells = to_table(cell[...].astype(f32)).astype(jnp.int32)
    volumes = weights * ((4.0 * math.pi / 3.0) * reach * reach * reach)
    for c in range(3):
        velocity_out[c * SLOTS : (c + 1) * SLOTS] = parts[c]
    cell_out[...] = cells
    amounts = [volumes] + [volumes * part for part in parts]
    highs = [amount.astype(bf16).astype(f32) for amount in amounts]
    lows = [amount - high for amount, high in zip(amounts, highs)]
    rows = lax.broadcasted_iota(jnp.int32, (16, CLUSTERS), 0).astype(f32).astype(bf16)
    total = jnp.zeros((2 * 4 * 16, LANES), f32)
    for slot in range(SLOTS):
        cell_row = cells[slot : slot + 1]
        hot = one_hot(cell_row & (LANES - 1), LANES)
        group = rows == (cell_row >> 7).astype(f32).astype(bf16)
        spread = [
            jnp.where(group, part[slot : slot + 1].astype(bf16), jnp.zeros((), bf16))
            for part in highs + lows
        ]
        total = total + dot_lanes(jnp.concatenate(spread, axis=0), hot)
    total = total[:64] + total[64:]
    totals_out[...] = total
    parcels = []
    for owner in range(16):
        span = slice(owner * LANES, (owner + 1) * LANES)
        parcels.append(
            jnp.concatenate(
                [total[c * 16 + owner : c * 16 + owner + 1] for c in range(4)]
                + [fluid[:, span] + time_step * pressure[:, span], jnp.zeros((1, LANES), f32)],
                axis=0,
            )
        )
    part_parcels(parcels, 1, stay, away)


def fluid_kernel(totals, stay, got, cell, at_grain, parcels_out, stage):
    parcels = join_parcels(stay, got, 8)
    for source in range(16):
        parcels_out[source] = parcels[source]
    volume = totals[:16]
    void_here = jnp.maximum(1.0 - volume / cell_volume, void_floor)
    drag_rate = drag_factor * (1.1 - void_here) / (void_here * void_here)
    below = void_here + time_step * drag_rate * volume / cell_volume
    fields = []
    for c in range(3):
        momentum = drag_rate * totals[(c + 1) * 16 : (c + 2) * 16] / cell_volume
        driven = jnp.concatenate([parcels[k][4 + c : 5 + c] for k in range(16)], axis=0)
        fields.append((void_here * driven + time_step * momentum) / below)
    fields.append(drag_rate)
    mixed = jnp.concatenate(
        [field[k : k + 1] for k in range(16) for field in fields], axis=0
    )
    parts = jnp.concatenate(split(mixed, 2), axis=0)
    ranges = lax.broadcasted_iota(jnp.int32, (64, CLUSTERS), 0) >> 2
    for slot in range(SLOTS):
        cell_row = cell[slot : slot + 1, :]
        seen = dot(parts, one_hot(cell_row & (LANES - 1), LANES))
        chosen = jnp.where(ranges == (cell_row >> 7), seen[:64] + seen[64:], 0.0)
        found = chosen[:8]
        for k in range(1, 8):
            found = found + chosen[8 * k : 8 * (k + 1)]
        found = found[:4] + found[4:]
        for k in range(GROUP):
            row = k * LANES + slot * 4
            stage[row : row + 4, :] = found[:, k * LANES : (k + 1) * LANES]
    for c in range(4):
        for k in range(GROUP):
            at_grain[c * SLOTS : (c + 1) * SLOTS, k * LANES : (k + 1) * LANES] = stage[
                pl.ds(k * LANES + c, SLOTS, stride=4), :
            ]


def owned_kernel(parcels, fluid, pressure, fluid_out, void_out):
    for source in range(16):
        span = slice(source * LANES, (source + 1) * LANES)
        volume = parcels[source, 0:1, :]
        void_here = jnp.maximum(1.0 - volume / cell_volume, void_floor)
        drag_rate = drag_factor * (1.1 - void_here) / (void_here * void_here)
        below = void_here + time_step * drag_rate * volume / cell_volume
        push = void_here * pressure[:, span] + drag_rate * parcels[source, 1:4, :] / cell_volume
        fluid_out[:, span] = (void_here * fluid[:, span] + time_step * push) / below
        void_out[source : source + 1, :] = void_here


def advance(state, velocity, reach, at_grain, force, middle, got_lead, got_trail, hot):
    low = lower_half((3 * SLOTS, LANES))
    from_last, from_next = by_parity("gy", got_lead[...], got_trail[...])
    last_whole, last_half = unfold(from_last, False)
    next_whole, next_half = unfold(from_next, True)
    tiles = [
        last_whole,
        jnp.where(low, last_half, middle[...]),
        jnp.where(low, middle[...], next_half),
        next_whole,
    ]
    tiles = [jnp.where(present_tile(2 * k, 2 * k + 1), tiles[k], 0.0) for k in range(4)]
    returned = jnp.concatenate(tiles, axis=1)
    added = dot_lanes(jnp.concatenate(split(returned, 2), axis=0), hot[...])
    contact = spring * (force[...] - (added[: 3 * SLOTS] + added[3 * SLOTS :]))
    weights = state[3 * SLOTS :, :]
    sphere = (4.0 * math.pi / 3.0) * reach * reach * reach
    masses = grain_density * sphere
    volumes = weights * sphere
    drag = at_grain[3 * SLOTS :, :] * volumes
    places, speeds = [], []
    for c in range(3):
        rows = slice(c * SLOTS, (c + 1) * SLOTS)
        speed = velocity[rows, :]
        pull = (contact[rows] + drag * (at_grain[rows, :] - speed)) / masses
        if c == 2:
            pull = pull - gravity
        speed = speed + time_step * weights * pull
        speeds.append(speed)
        places.append(state[rows, :] + time_step * weights * speed)
    return places, speeds, weights


def middle_kernel(
    table, state, velocity, at_grain, force, middle, got_lead, got_trail, hot,
    table_out, state_out, velocity_out, lead, trail, middle_out,
):
    reach = table[3 * SLOTS :, :]
    places, speeds, weights = advance(
        state, velocity, reach, at_grain, force, middle, got_lead, got_trail, hot
    )
    real = weights > 0.5
    moved = jnp.concatenate([jnp.where(real, place, FAR) for place in places] + [reach], axis=0)
    table_out[...] = moved
    for c in range(3):
        state_out[c * SLOTS : (c + 1) * SLOTS] = places[c]
        velocity_out[c * SLOTS : (c + 1) * SLOTS] = speeds[c]
    state_out[3 * SLOTS :] = weights
    send_pieces(moved, 3 * SLOTS, hot, lead, trail, middle_out)


def last_kernel(
    table, state, velocity, at_grain, force, middle, got_lead, got_trail, hot,
    positions_out, velocity_out, stage,
):
    places, speeds, _ = advance(
        state, velocity, table[3 * SLOTS :, :], at_grain, force, middle, got_lead, got_trail, hot
    )
    store_components(positions_out, stage, jnp.concatenate(places, axis=0))
    store_components(velocity_out, stage, jnp.concatenate(speeds, axis=0))


def snake(array, axis, sign):
    size_x, size_y = lax.axis_size("gx"), lax.axis_size("gy")
    moves = []
    for x in range(size_x):
        for y in range(size_y):
            if axis == "gx":
                target = (x + (sign if y % 2 == 0 else -sign), y)
                target = target if 0 <= target[0] < size_x else (x, y ^ 1)
            else:
                target = (x, y + (sign if x % 2 == 0 else -sign))
                target = target if 0 <= target[1] < size_y else (x ^ 1, y)
            moves.append((x * size_y + y, target[0] * size_y + target[1]))
    return lax.ppermute(array, ("gx", "gy"), moves)


def swap(array, bit):
    size_x, size_y = lax.axis_size("gx"), lax.axis_size("gy")
    moves = [(x * size_y + y, x * size_y + (y ^ bit)) for x in range(size_x) for y in range(size_y)]
    return lax.ppermute(array, ("gx", "gy"), moves)


def table_shape(rows, columns=CLUSTERS):
    return jax.ShapeDtypeStruct((rows, columns), f32)


STAGE = pltpu.VMEM((3 * CHUNKS, LANES), f32)
HOT = jax.ShapeDtypeStruct((CLUSTERS, PAIRS), bf16)
SLOT_ROWS = table_shape(4 * SLOTS * 8, LANES)
FORCE_ROWS = table_shape(3 * SLOTS * 8, LANES)
FORCE_SCRATCH = pltpu.VMEM((3 * SLOTS * 8, LANES), f32)
PARCELS = jax.ShapeDtypeStruct((8, 8, LANES), f32)


def call(kernel, out_shape, operands, scratch=(), cost=1.0, far=False, after=()):
    count = len(operands)

    def body(*refs):
        kernel(*refs[:count], *refs[count + len(after) :])

    space = pltpu.HBM if far else pltpu.VMEM
    if far:
        operands = tuple(pltpu.with_memory_space_constraint(array, pltpu.HBM) for array in operands)
    return pl.pallas_call(
        body,
        out_shape=out_shape,
        in_specs=[pl.BlockSpec(memory_space=space)] * count
        + [pl.BlockSpec(memory_space=pl.ANY)] * len(after),
        scratch_shapes=list(scratch),
        compiler_params=PARAMS,
        cost_estimate=pl.CostEstimate(
            flops=int(cost * 10**9), bytes_accessed=int(cost * 10**6), transcendentals=0
        ),
        name=kernel.__name__,
    )(*operands, *after)


def shards(
    positions,
    velocity,
    radius,
    grain_mask,
    grain_cell,
    inner_pairs,
    cross_pairs,
    send_lists,
    fluid_velocity,
    pressure_grad,
):
    send = send_lists.reshape(1, -1)
    radius = radius.reshape(CHUNKS, LANES)
    mask = grain_mask.reshape(CHUNKS, LANES)
    cell = grain_cell.reshape(CHUNKS, LANES)

    full, wide = table_shape(4 * SLOTS), table_shape(6 * SLOTS, LANES)
    narrow, single = table_shape(9 * SLOTS // 2, LANES), table_shape(3 * SLOTS, LANES)
    three, full_tile = table_shape(3 * SLOTS), table_shape(4 * SLOTS, LANES)

    def near(array):
        return pltpu.VMEM(array.shape, array.dtype)

    def like(array):
        return jax.ShapeDtypeStruct(array.shape, array.dtype)

    needed = (positions, radius, mask, send)
    later = (velocity, cell, fluid_velocity, pressure_grad, inner_pairs, cross_pairs)
    table, state, hot, lead, trail, middle, *later = call(
        prepare,
        (
            full,
            full,
            jax.ShapeDtypeStruct((CLUSTERS, CLUSTERS), bf16),
            wide,
            wide,
            full_tile,
            *[like(array) for array in later],
        ),
        needed + later,
        [near(array) for array in needed] + [STAGE, pltpu.SemaphoreType.DMA((10,))],
        far=True,
    )
    velocity, cell, fluid, pressure, inner_pairs, cross_pairs = later
    moving, cells, totals, stay, away = call(
        deposit_kernel,
        (
            three,
            jax.ShapeDtypeStruct((SLOTS, CLUSTERS), jnp.int32),
            table_shape(64, LANES),
            PARCELS,
            PARCELS,
        ),
        (table, state, velocity, cell, fluid, pressure),
        [STAGE],
        3,
    )
    got = swap(away, 1)

    cross_scratch = [pltpu.VMEM(SLOT_ROWS.shape, f32), FORCE_SCRATCH]
    for substep in range(2):
        first = substep == 0
        got_lead, got_trail = snake(lead, "gx", 1), snake(trail, "gx", -1)
        if not first:
            rows = call(
                inner_again,
                (SLOT_ROWS, SLOT_ROWS, FORCE_ROWS, FORCE_ROWS),
                (table, inner_pairs, hot_a, hot_b),
                cost=3,
            )
        lead, trail, side = call(
            pass_ghosts,
            (wide, wide, full_tile) if first else (narrow, narrow, single),
            (got_lead, got_trail, middle),
            after=(away,) if first else (rows[3],),
        )
        got_lead, got_trail = snake(lead, "gy", 1), snake(trail, "gy", -1)
        if first:
            stay, away = call(relay(1), (PARCELS, PARCELS), (stay, got), after=(lead, trail))
            got = swap(away, 2)
            hot_a, hot_b, *rows = call(
                inner_start,
                (HOT, HOT, SLOT_ROWS, SLOT_ROWS, FORCE_ROWS, FORCE_ROWS),
                (table, inner_pairs),
                cost=3,
                after=(away,),
            )
            hot_c, hot_d, leading = call(
                cross_start, (HOT, HOT, SLOT_ROWS), (table, cross_pairs), after=(rows[3],)
            )
            stay, away = call(relay(2), (PARCELS, PARCELS), (stay, got), after=(leading,))
            got = swap(away, 4)
            on_crossing, lead, trail, side, reach = call(
                cross_kernel,
                (FORCE_ROWS, narrow, narrow, single, table_shape(SLOTS)),
                (leading, hot_d, got_lead, got_trail, side),
                cross_scratch,
                4,
                after=(away,),
            )
        else:
            leading = call(
                cross_again, SLOT_ROWS, (table, cross_pairs, hot_c), after=(lead, trail)
            )
            sums = call(inner_rest, (FORCE_ROWS, FORCE_ROWS), rows, cost=2, after=(leading,))
            on_crossing, lead, trail, side = call(
                cross_kernel_again,
                (FORCE_ROWS, narrow, narrow, single),
                (leading, hot_d, got_lead, got_trail, side, reach),
                cross_scratch,
                4,
                after=(sums[1],),
            )
        got_lead, got_trail = snake(lead, "gy", 1), snake(trail, "gy", -1)
        if first:
            stay, away = call(relay(4), (PARCELS, PARCELS), (stay, got), after=(side,))
            got = swap(away, 8)
            sums = call(inner_rest, (FORCE_ROWS, FORCE_ROWS), rows, cost=2, after=(away,))
        force = call(
            scatter_kernel, three, (*sums, on_crossing, hot_a, hot_b, hot_c), cost=2, after=(side,)
        )
        lead, trail, middle = call(
            pass_forces, (narrow, narrow, single), (got_lead, got_trail, side), after=(force,)
        )
        got_lead, got_trail = snake(lead, "gx", 1), snake(trail, "gx", -1)
        if first:
            at_grain, parcels = call(
                fluid_kernel,
                (full, jax.ShapeDtypeStruct((16, 8, LANES), f32)),
                (totals, stay, got, cells),
                [pltpu.VMEM((GROUP * LANES, LANES), f32)],
                3,
                after=(lead, trail),
            )
        else:
            fluid_out, void_out = call(
                owned_kernel,
                (like(fluid_velocity), table_shape(16, LANES)),
                (parcels, fluid, pressure),
                after=(lead, trail),
            )
        operands = (table, state, moving, at_grain, force, middle, got_lead, got_trail, hot)
        if first:
            table, state, moving, lead, trail, middle = call(
                middle_kernel, (full, full, three, narrow, narrow, single), operands
            )
        else:
            positions, velocity = call(
                last_kernel, (like(positions), like(positions)), operands, [STAGE]
            )
    return positions, velocity, fluid_out, void_out.reshape(-1)


def solution(mesh):
    placed = (
        P(None, ("gx", "gy")),
        P(None, ("gx", "gy")),
        P(("gx", "gy")),
        P(("gx", "gy")),
        P(("gx", "gy")),
        P(None, ("gx", "gy")),
        P(None, ("gx", "gy")),
        P(("gx", "gy")),
        P(None, ("gx", "gy")),
        P(None, ("gx", "gy")),
    )
    return jax.shard_map(
        shards,
        mesh=mesh,
        in_specs=placed,
        out_specs=(
            P(None, ("gx", "gy")),
            P(None, ("gx", "gy")),
            P(None, ("gx", "gy")),
            P(("gx", "gy")),
        ),
        check_vma=False,
    )
```

```python
import math

import jax
import jax.numpy as jnp
from jax import lax
from jax.experimental import pallas as pl
from jax.experimental.pallas import tpu as pltpu
from jax.sharding import PartitionSpec as P

SLOTS = 32
LANES = 128
CLUSTERS = 512
GHOSTS = 64
PAIRS = 1024
CHUNKS = 128
GROUP = 4
NEIGHBOURS = ((-1, -1), (-1, 0), (-1, 1), (0, -1), (0, 1), (1, -1), (1, 0), (1, 1))
GHOST_ORDER = (7, 2, 3, 4, 5, 0, 1, 6)
PAIRED = ("gx", "gy")
OTHER = {"gx": "gy", "gy": "gx"}
BITS = (1, 4, 2, 8)
FAR = 2.0**30

spring = 4.0
time_step = 0.1
grain_density = 2.65
gravity = 1.0
cell_volume = 4.0
void_floor = 0.35
drag_factor = 0.5

f32 = jnp.float32
bf16 = jnp.bfloat16
PARAMS = pltpu.CompilerParams(vmem_limit_bytes=24 * 1024 * 1024)


def split(values, parts):
    pieces = []
    for _ in range(parts - 1):
        piece = values.astype(bf16)
        pieces.append(piece)
        values = values - piece.astype(f32)
    pieces.append(values.astype(bf16))
    return pieces


def one_hot(index_row, count):
    width = index_row.shape[1]
    rows = lax.broadcasted_iota(jnp.int32, (LANES, width), 0).astype(f32).astype(bf16)
    blocks = []
    for k in range(count // LANES):
        within = index_row - k * LANES
        within = jnp.where((within >= 0) & (within < LANES), within, -1).astype(f32).astype(bf16)
        blocks.append(jnp.where(rows == within, jnp.ones((), bf16), jnp.zeros((), bf16)))
    return jnp.concatenate(blocks, axis=0) if len(blocks) > 1 else blocks[0]


def dot(left, right):
    return jnp.dot(left, right, preferred_element_type=f32)


def dot_lanes(left, right):
    return lax.dot_general(left, right, (((1,), (1,)), ((), ())), preferred_element_type=f32)


def cluster_column(index):
    return (index & (GROUP - 1)) * LANES + (index >> 2)


def ghost_column(slot):
    block = slot >> 6
    column = jnp.zeros_like(slot)
    for position, offset in enumerate(GHOST_ORDER):
        column = jnp.where(block == offset, position * GHOSTS, column)
    return column + (slot & (GHOSTS - 1))


def lower_half(shape):
    return lax.broadcasted_iota(jnp.int32, shape, 1) < GHOSTS


def swap_halves(tile):
    return jnp.concatenate([tile[:, GHOSTS:], tile[:, :GHOSTS]], axis=1)


def fold(whole, half, upper):
    rows = half.shape[0] // 2
    low = lower_half((rows, LANES))
    if upper:
        packed = jnp.where(low, swap_halves(half[:rows]), half[rows:])
    else:
        packed = jnp.where(low, half[:rows], swap_halves(half[rows:]))
    return jnp.concatenate([whole, packed], axis=0)


def unfold(folded, upper):
    rows = folded.shape[0] // 3
    packed = folded[2 * rows :]
    turned = swap_halves(packed)
    half = [turned, packed] if upper else [packed, turned]
    return folded[: 2 * rows], jnp.concatenate(half, axis=0)


def by_parity(axis, even_first, even_second):
    even = lax.axis_index(axis) % 2 == 0
    return (
        jnp.where(even, even_first, even_second),
        jnp.where(even, even_second, even_first),
    )


def outgoing(axis, up, down):
    if axis in PAIRED:
        return by_parity(axis, down, up)
    return by_parity(OTHER[axis], up, down)


def incoming(axis, lead, trail):
    return by_parity(axis if axis in PAIRED else OTHER[axis], lead, trail)


def to_table(square):
    turned = square.T
    return jnp.concatenate([turned[k * SLOTS : (k + 1) * SLOTS] for k in range(GROUP)], axis=1)


def from_table(table):
    stacked = jnp.concatenate([table[:, k * LANES : (k + 1) * LANES] for k in range(GROUP)], axis=0)
    return stacked.T


def load_components(ref, stage):
    for i in range(CHUNKS):
        stage[pl.ds(i, 3, stride=CHUNKS), :] = ref[:, i * LANES : (i + 1) * LANES]
    return [to_table(stage[c * CHUNKS : (c + 1) * CHUNKS, :]) for c in range(3)]


def store_components(ref, stage, table):
    for c in range(3):
        stage[c * CHUNKS : (c + 1) * CHUNKS, :] = from_table(table[c * SLOTS : (c + 1) * SLOTS])
    for i in range(CHUNKS):
        ref[:, i * LANES : (i + 1) * LANES] = stage[pl.ds(i, 3, stride=CHUNKS), :]


def gather(table_parts, hot, rows):
    picked = dot(table_parts, hot)
    total = picked[:rows]
    for k in range(1, table_parts.shape[0] // rows):
        total = total + picked[k * rows : (k + 1) * rows]
    return total


def send_pieces(table, rows, hot, lead, trail, middle):
    pieces = gather(jnp.concatenate(split(table[:rows], 3), axis=0), hot[...], rows)
    tiles = [pieces[:, k * LANES : (k + 1) * LANES] for k in range(4)]
    up = fold(tiles[3], tiles[2], True)
    down = fold(tiles[0], tiles[1], False)
    lead[...], trail[...] = outgoing("gx", up, down)
    middle[...] = jnp.where(lower_half(tiles[1].shape), tiles[2], tiles[1])


def start_copies(pairs, arrived, first=0):
    copies = [
        pltpu.make_async_copy(far, near, arrived.at[first + k])
        for k, (far, near) in enumerate(pairs)
    ]
    for copy in copies:
        copy.start()
    return copies


def prepare(
    positions_far, radius_far, mask_far, send_far,
    velocity_far, cell_far, fluid_far, pressure_far, inner_far, cross_far,
    table_out, state_out, hot, lead, trail, middle, velocity, cell, fluid, pressure, inner, cross,
    positions, radius, mask, send, stage, arrived,
):
    needed = start_copies(
        ((positions_far, positions), (radius_far, radius), (mask_far, mask), (send_far, send)), arrived
    )
    later = start_copies(
        (
            (velocity_far, velocity),
            (cell_far, cell),
            (fluid_far, fluid),
            (pressure_far, pressure),
            (inner_far, inner),
            (cross_far, cross),
        ),
        arrived,
        4,
    )
    for copy in needed:
        copy.wait()
    parts = load_components(positions, stage)
    reach = to_table(radius[...])
    weights = to_table(mask[...].astype(f32))
    real = weights > 0.5
    table = jnp.concatenate([jnp.where(real, part, FAR) for part in parts] + [reach], axis=0)
    table_out[...] = table
    for c in range(3):
        state_out[c * SLOTS : (c + 1) * SLOTS] = parts[c]
    state_out[3 * SLOTS :] = weights
    hot[...] = one_hot(cluster_column(send[...]), CLUSTERS)
    send_pieces(table, 4 * SLOTS, hot, lead, trail, middle)
    for copy in later:
        copy.wait()


def contacts(leading, partner, on_leading, on_partner, begin, end):
    step = 4

    def row(component, slot):
        return pl.ds(pl.multiple_of((component * SLOTS + slot) * 8, 8), 8)

    def some_slots(block, carry):
        base = block * step
        ours = [[leading[row(c, base + i), :] for c in range(4)] for i in range(step)]
        sums = [[jnp.zeros((8, LANES), f32) for _ in range(3)] for _ in range(step)]
        for q in range(SLOTS):
            theirs = [partner[row(c, q), :] for c in range(4)]
            back = [on_partner[row(c, q), :] for c in range(3)]
            for i in range(step):
                apart = [ours[i][c] - theirs[c] for c in range(3)]
                squared = apart[0] * apart[0] + apart[1] * apart[1] + apart[2] * apart[2]
                reach = ours[i][3] + theirs[3]
                weight = jnp.maximum(reach * reach - squared, 0.0)
                for c in range(3):
                    push = weight * apart[c]
                    sums[i][c] = sums[i][c] + push
                    back[c] = back[c] + push
            for c in range(3):
                on_partner[row(c, q), :] = back[c]
        for i in range(step):
            for c in range(3):
                on_leading[row(c, base + i), :] = sums[i][c]
        return carry

    lax.fori_loop(begin // step, end // step, some_slots, 0)


def fill_hot(pairs, row, column, hot):
    width = 2 * LANES
    for block in range(PAIRS // width):
        span = slice(block * width, (block + 1) * width)
        hot[:, span] = one_hot(column(pairs[row : row + 1, span]), CLUSTERS)


def fill_slots(parts, hot, pairs, landed):
    width = 2 * LANES
    for block in range(PAIRS // width):
        span = slice(block * width, (block + 1) * width)
        picked = gather(parts, hot[:, span], 4 * SLOTS)
        if pairs is not None:
            offsets = pairs[2:5, span].astype(f32)
            picked = jnp.concatenate(
                [picked[c * SLOTS : (c + 1) * SLOTS] - offsets[c : c + 1] for c in range(3)]
                + [picked[3 * SLOTS :]],
                axis=0,
            )
        for k in range(2):
            landed[pl.ds(2 * block + k, 4 * SLOTS, stride=8), :] = picked[
                :, k * LANES : (k + 1) * LANES
            ]


def scatter(sums, hot):
    pieces = jnp.concatenate(
        [sums[pl.ds(k, 3 * SLOTS, stride=8), :] for k in range(PAIRS // LANES)], axis=1
    )
    added = dot_lanes(jnp.concatenate(split(pieces, 2), axis=0), hot[...])
    return added[: 3 * SLOTS] + added[3 * SLOTS :]


def table_parts(table):
    return jnp.concatenate(split(table[...], 2), axis=0)


INNER_SPLIT = 16


def inner_start(table, pairs, hot_a, hot_b, leading, partner, on_leading, on_partner):
    fill_hot(pairs, 0, cluster_column, hot_a)
    fill_hot(pairs, 1, cluster_column, hot_b)
    inner_again(table, pairs, hot_a, hot_b, leading, partner, on_leading, on_partner)


def inner_again(table, pairs, hot_a, hot_b, leading, partner, on_leading, on_partner):
    parts = table_parts(table)
    fill_slots(parts, hot_a, pairs, leading)
    fill_slots(parts, hot_b, None, partner)
    on_partner[...] = jnp.zeros_like(on_partner)
    contacts(leading, partner, on_leading, on_partner, 0, INNER_SPLIT)
    for c in range(3):
        later = slice((c * SLOTS + INNER_SPLIT) * 8, (c + 1) * SLOTS * 8)
        on_leading[later, :] = jnp.zeros(((SLOTS - INNER_SPLIT) * 8, LANES), f32)


def inner_rest(leading, partner, on_leading_first, on_partner_first, on_leading, on_partner):
    for c in range(3):
        done = slice(c * SLOTS * 8, (c * SLOTS + INNER_SPLIT) * 8)
        on_leading[done, :] = on_leading_first[done, :]
    on_partner[...] = on_partner_first[...]
    contacts(leading, partner, on_leading, on_partner, INNER_SPLIT, SLOTS)


def cross_start(table, pairs, hot_a, hot_b, leading):
    fill_hot(pairs, 0, cluster_column, hot_a)
    fill_hot(pairs, 1, ghost_column, hot_b)
    cross_again(table, pairs, hot_a, leading)


def cross_again(table, pairs, hot_a, leading):
    fill_slots(table_parts(table), hot_a, pairs, leading)


def scatter_kernel(on_leading, on_partner, on_crossing, hot_a, hot_b, hot_c, force):
    force[...] = (
        scatter(on_leading, hot_a) - scatter(on_partner, hot_b) + scatter(on_crossing, hot_c)
    )


def present_tile(low, high):
    here_x, here_y = lax.axis_index("gx"), lax.axis_index("gy")
    flags = []
    for slot in (low, high):
        a, b = NEIGHBOURS[slot]
        x, y = here_x + a, here_y + b
        inside = (x >= 0) & (x < lax.axis_size("gx")) & (y >= 0) & (y < lax.axis_size("gy"))
        flags.append(jnp.where(inside, 1, 0))
    return jnp.where(lower_half((1, LANES)), flags[0], flags[1]) > 0


def pass_ghosts(got_lead, got_trail, middle, lead_out, trail_out, side):
    low = lower_half(middle.shape)
    from_last, from_next = incoming("gx", got_lead[...], got_trail[...])
    last_whole, last_half = unfold(from_last, True)
    next_whole, next_half = unfold(from_next, False)
    minus = fold(jnp.where(low, next_whole, last_half), middle[...], True)
    plus = fold(jnp.where(low, next_half, last_whole), middle[...], False)
    lead_out[...], trail_out[...] = outgoing("gy", plus, minus)
    side[...] = jnp.where(low, last_whole, next_whole)


def cross_contacts(ghosts, leading, hot_b, on_leading, lead, trail, side_out, partner, on_partner):
    fill_slots(table_parts(ghosts), hot_b, None, partner)
    on_partner[...] = jnp.zeros_like(on_partner)
    contacts(leading, partner, on_leading, on_partner, 0, SLOTS)
    back = scatter(on_partner, hot_b)
    tiles = [back[:, k * LANES : (k + 1) * LANES] for k in range(4)]
    up = fold(tiles[0], tiles[1], True)
    down = fold(tiles[2], tiles[1], False)
    lead[...], trail[...] = outgoing("gy", up, down)
    side_out[...] = tiles[3]


def ghost_places(got_lead, got_trail, side):
    from_last, from_next = incoming("gy", got_lead[...], got_trail[...])
    last_whole, last_half = unfold(from_last, False)
    next_whole, next_half = unfold(from_next, True)
    low = lower_half(side.shape)
    tiles = [next_whole, jnp.where(low, last_half, next_half), last_whole, side[...]]
    placed = [
        jnp.where(
            present_tile(GHOST_ORDER[2 * k], GHOST_ORDER[2 * k + 1]), tiles[k][: 3 * SLOTS], FAR
        )
        for k in range(4)
    ]
    return tiles, jnp.concatenate(placed, axis=1)


def cross_kernel(
    leading, hot_b, got_lead, got_trail, side,
    on_leading, lead, trail, side_out, reach_out, partner, on_partner,
):
    tiles, placed = ghost_places(got_lead, got_trail, side)
    reach = jnp.concatenate([tile[3 * SLOTS :] for tile in tiles], axis=1)
    reach_out[...] = reach
    ghosts = jnp.concatenate([placed, reach], axis=0)
    cross_contacts(ghosts, leading, hot_b, on_leading, lead, trail, side_out, partner, on_partner)


def cross_kernel_again(
    leading, hot_b, got_lead, got_trail, side, reach,
    on_leading, lead, trail, side_out, partner, on_partner,
):
    _, placed = ghost_places(got_lead, got_trail, side)
    ghosts = jnp.concatenate([placed, reach[...]], axis=0)
    cross_contacts(ghosts, leading, hot_b, on_leading, lead, trail, side_out, partner, on_partner)


def pass_forces(got_lead, got_trail, side, lead_out, trail_out, middle):
    low = lower_half((3 * SLOTS, LANES))
    from_last, from_next = incoming("gy", got_lead[...], got_trail[...])
    last_whole, last_half = unfold(from_last, True)
    next_whole, next_half = unfold(from_next, False)
    up = fold(jnp.where(low, last_whole, side[...]), next_whole, False)
    down = fold(jnp.where(low, side[...], next_whole), last_whole, True)
    lead_out[...], trail_out[...] = outgoing("gx", up, down)
    middle[...] = jnp.where(low, next_half, last_half)


def part_parcels(parcels, bit, stay, away):
    mine = (lax.axis_index("gy") & bit) > 0
    for k, low in enumerate([d for d in range(16) if not d & bit]):
        stay[k] = jnp.where(mine, parcels[low | bit], parcels[low])
        away[k] = jnp.where(mine, parcels[low], parcels[low | bit])


def join_parcels(stay, got, bit):
    mine = (lax.axis_index("gy") & bit) > 0
    parcels = [None] * 16
    for k, low in enumerate([d for d in range(16) if not d & bit]):
        parcels[low] = jnp.where(mine, got[k], stay[k])
        parcels[low | bit] = jnp.where(mine, stay[k], got[k])
    return parcels


def relay(step):
    def relay_parcels(stay, got, stay_out, away_out):
        part_parcels(join_parcels(stay, got, BITS[step]), BITS[step + 1], stay_out, away_out)

    return relay_parcels


def deposit_kernel(
    table, state, velocity, cell, fluid, pressure, velocity_out, cell_out, totals_out, stay, away, stage
):
    parts = load_components(velocity, stage)
    reach = table[3 * SLOTS :, :]
    weights = state[3 * SLOTS :, :]
    cells = to_table(cell[...].astype(f32)).astype(jnp.int32)
    volumes = weights * ((4.0 * math.pi / 3.0) * reach * reach * reach)
    for c in range(3):
        velocity_out[c * SLOTS : (c + 1) * SLOTS] = parts[c]
    cell_out[...] = cells
    amounts = [volumes] + [volumes * part for part in parts]
    highs = [amount.astype(bf16).astype(f32) for amount in amounts]
    lows = [amount - high for amount, high in zip(amounts, highs)]
    rows = lax.broadcasted_iota(jnp.int32, (16, CLUSTERS), 0).astype(f32).astype(bf16)
    total = jnp.zeros((2 * 4 * 16, LANES), f32)
    for slot in range(SLOTS):
        cell_row = cells[slot : slot + 1]
        hot = one_hot(cell_row & (LANES - 1), LANES)
        group = rows == (cell_row >> 7).astype(f32).astype(bf16)
        spread = [
            jnp.where(group, part[slot : slot + 1].astype(bf16), jnp.zeros((), bf16))
            for part in highs + lows
        ]
        total = total + dot_lanes(jnp.concatenate(spread, axis=0), hot)
    total = total[:64] + total[64:]
    totals_out[...] = total
    parcels = []
    for owner in range(16):
        span = slice(owner * LANES, (owner + 1) * LANES)
        parcels.append(
            jnp.concatenate(
                [total[c * 16 + owner : c * 16 + owner + 1] for c in range(4)]
                + [fluid[:, span] + time_step * pressure[:, span], jnp.zeros((1, LANES), f32)],
                axis=0,
            )
        )
    part_parcels(parcels, BITS[0], stay, away)


def fluid_kernel(totals, stay, got, cell, at_grain, parcels_out, stage):
    parcels = join_parcels(stay, got, BITS[3])
    for source in range(16):
        parcels_out[source] = parcels[source]
    volume = totals[:16]
    void_here = jnp.maximum(1.0 - volume / cell_volume, void_floor)
    drag_rate = drag_factor * (1.1 - void_here) / (void_here * void_here)
    below = void_here + time_step * drag_rate * volume / cell_volume
    fields = []
    for c in range(3):
        momentum = drag_rate * totals[(c + 1) * 16 : (c + 2) * 16] / cell_volume
        driven = jnp.concatenate([parcels[k][4 + c : 5 + c] for k in range(16)], axis=0)
        fields.append((void_here * driven + time_step * momentum) / below)
    fields.append(drag_rate)
    mixed = jnp.concatenate(
        [field[k : k + 1] for k in range(16) for field in fields], axis=0
    )
    parts = jnp.concatenate(split(mixed, 2), axis=0)
    ranges = lax.broadcasted_iota(jnp.int32, (64, CLUSTERS), 0) >> 2
    for slot in range(SLOTS):
        cell_row = cell[slot : slot + 1, :]
        seen = dot(parts, one_hot(cell_row & (LANES - 1), LANES))
        chosen = jnp.where(ranges == (cell_row >> 7), seen[:64] + seen[64:], 0.0)
        found = chosen[:8]
        for k in range(1, 8):
            found = found + chosen[8 * k : 8 * (k + 1)]
        found = found[:4] + found[4:]
        for k in range(GROUP):
            row = k * LANES + slot * 4
            stage[row : row + 4, :] = found[:, k * LANES : (k + 1) * LANES]
    for c in range(4):
        for k in range(GROUP):
            at_grain[c * SLOTS : (c + 1) * SLOTS, k * LANES : (k + 1) * LANES] = stage[
                pl.ds(k * LANES + c, SLOTS, stride=4), :
            ]


def owned_kernel(parcels, fluid, pressure, fluid_out, void_out):
    for source in range(16):
        span = slice(source * LANES, (source + 1) * LANES)
        volume = parcels[source, 0:1, :]
        void_here = jnp.maximum(1.0 - volume / cell_volume, void_floor)
        drag_rate = drag_factor * (1.1 - void_here) / (void_here * void_here)
        below = void_here + time_step * drag_rate * volume / cell_volume
        push = void_here * pressure[:, span] + drag_rate * parcels[source, 1:4, :] / cell_volume
        fluid_out[:, span] = (void_here * fluid[:, span] + time_step * push) / below
        void_out[source : source + 1, :] = void_here


def advance(state, velocity, reach, at_grain, force, middle, got_lead, got_trail, hot):
    low = lower_half((3 * SLOTS, LANES))
    from_last, from_next = incoming("gx", got_lead[...], got_trail[...])
    last_whole, last_half = unfold(from_last, False)
    next_whole, next_half = unfold(from_next, True)
    tiles = [
        last_whole,
        jnp.where(low, last_half, middle[...]),
        jnp.where(low, middle[...], next_half),
        next_whole,
    ]
    tiles = [jnp.where(present_tile(2 * k, 2 * k + 1), tiles[k], 0.0) for k in range(4)]
    returned = jnp.concatenate(tiles, axis=1)
    added = dot_lanes(jnp.concatenate(split(returned, 2), axis=0), hot[...])
    contact = spring * (force[...] - (added[: 3 * SLOTS] + added[3 * SLOTS :]))
    weights = state[3 * SLOTS :, :]
    sphere = (4.0 * math.pi / 3.0) * reach * reach * reach
    masses = grain_density * sphere
    volumes = weights * sphere
    drag = at_grain[3 * SLOTS :, :] * volumes
    places, speeds = [], []
    for c in range(3):
        rows = slice(c * SLOTS, (c + 1) * SLOTS)
        speed = velocity[rows, :]
        pull = (contact[rows] + drag * (at_grain[rows, :] - speed)) / masses
        if c == 2:
            pull = pull - gravity
        speed = speed + time_step * weights * pull
        speeds.append(speed)
        places.append(state[rows, :] + time_step * weights * speed)
    return places, speeds, weights


def middle_kernel(
    table, state, velocity, at_grain, force, middle, got_lead, got_trail, hot,
    table_out, state_out, velocity_out, lead, trail, middle_out,
):
    reach = table[3 * SLOTS :, :]
    places, speeds, weights = advance(
        state, velocity, reach, at_grain, force, middle, got_lead, got_trail, hot
    )
    real = weights > 0.5
    moved = jnp.concatenate([jnp.where(real, place, FAR) for place in places] + [reach], axis=0)
    table_out[...] = moved
    for c in range(3):
        state_out[c * SLOTS : (c + 1) * SLOTS] = places[c]
        velocity_out[c * SLOTS : (c + 1) * SLOTS] = speeds[c]
    state_out[3 * SLOTS :] = weights
    send_pieces(moved, 3 * SLOTS, hot, lead, trail, middle_out)


def last_kernel(
    table, state, velocity, at_grain, force, middle, got_lead, got_trail, hot,
    positions_out, velocity_out, stage,
):
    places, speeds, _ = advance(
        state, velocity, table[3 * SLOTS :, :], at_grain, force, middle, got_lead, got_trail, hot
    )
    store_components(positions_out, stage, jnp.concatenate(places, axis=0))
    store_components(velocity_out, stage, jnp.concatenate(speeds, axis=0))


def exchange(lead, trail, axis):
    size_x, size_y = lax.axis_size("gx"), lax.axis_size("gy")
    routes = ([], [])
    for x in range(size_x):
        for y in range(size_y):
            along, across = (x, y) if axis == "gx" else (y, x)
            last = (size_x if axis == "gx" else size_y) - 1
            up_first = along % 2 == 1 if axis in PAIRED else across % 2 == 0
            for route, step in zip(routes, (1, -1) if up_first else (-1, 1)):
                target = along + step
                ends = (target, across) if 0 <= target <= last else (along, across ^ 1)
                to_x, to_y = ends if axis == "gx" else ends[::-1]
                route.append((x * size_y + y, to_x * size_y + to_y))
    return tuple(
        lax.ppermute(block, ("gx", "gy"), route) for block, route in zip((lead, trail), routes)
    )


def swap(array, bit):
    size_x, size_y = lax.axis_size("gx"), lax.axis_size("gy")
    moves = [(x * size_y + y, x * size_y + (y ^ bit)) for x in range(size_x) for y in range(size_y)]
    return lax.ppermute(array, ("gx", "gy"), moves)


def table_shape(rows, columns=CLUSTERS):
    return jax.ShapeDtypeStruct((rows, columns), f32)


STAGE = pltpu.VMEM((3 * CHUNKS, LANES), f32)
HOT = jax.ShapeDtypeStruct((CLUSTERS, PAIRS), bf16)
SLOT_ROWS = table_shape(4 * SLOTS * 8, LANES)
FORCE_ROWS = table_shape(3 * SLOTS * 8, LANES)
FORCE_SCRATCH = pltpu.VMEM((3 * SLOTS * 8, LANES), f32)
PARCELS = jax.ShapeDtypeStruct((8, 8, LANES), f32)


def call(kernel, out_shape, operands, scratch=(), cost=1.0, far=False, after=()):
    count = len(operands)

    def body(*refs):
        kernel(*refs[:count], *refs[count + len(after) :])

    space = pltpu.HBM if far else pltpu.VMEM
    if far:
        operands = tuple(pltpu.with_memory_space_constraint(array, pltpu.HBM) for array in operands)
    return pl.pallas_call(
        body,
        out_shape=out_shape,
        in_specs=[pl.BlockSpec(memory_space=space)] * count
        + [pl.BlockSpec(memory_space=pl.ANY)] * len(after),
        scratch_shapes=list(scratch),
        compiler_params=PARAMS,
        cost_estimate=pl.CostEstimate(
            flops=int(cost * 10**9), bytes_accessed=int(cost * 10**6), transcendentals=0
        ),
        name=kernel.__name__,
    )(*operands, *after)


def shards(
    positions,
    velocity,
    radius,
    grain_mask,
    grain_cell,
    inner_pairs,
    cross_pairs,
    send_lists,
    fluid_velocity,
    pressure_grad,
):
    send = send_lists.reshape(1, -1)
    radius = radius.reshape(CHUNKS, LANES)
    mask = grain_mask.reshape(CHUNKS, LANES)
    cell = grain_cell.reshape(CHUNKS, LANES)

    full, wide = table_shape(4 * SLOTS), table_shape(6 * SLOTS, LANES)
    narrow, single = table_shape(9 * SLOTS // 2, LANES), table_shape(3 * SLOTS, LANES)
    three, full_tile = table_shape(3 * SLOTS), table_shape(4 * SLOTS, LANES)

    def near(array):
        return pltpu.VMEM(array.shape, array.dtype)

    def like(array):
        return jax.ShapeDtypeStruct(array.shape, array.dtype)

    needed = (positions, radius, mask, send)
    later = (velocity, cell, fluid_velocity, pressure_grad, inner_pairs, cross_pairs)
    table, state, hot, lead, trail, middle, *later = call(
        prepare,
        (
            full,
            full,
            jax.ShapeDtypeStruct((CLUSTERS, CLUSTERS), bf16),
            wide,
            wide,
            full_tile,
            *[like(array) for array in later],
        ),
        needed + later,
        [near(array) for array in needed] + [STAGE, pltpu.SemaphoreType.DMA((10,))],
        far=True,
    )
    velocity, cell, fluid, pressure, inner_pairs, cross_pairs = later
    moving, cells, totals, stay, away = call(
        deposit_kernel,
        (
            three,
            jax.ShapeDtypeStruct((SLOTS, CLUSTERS), jnp.int32),
            table_shape(64, LANES),
            PARCELS,
            PARCELS,
        ),
        (table, state, velocity, cell, fluid, pressure),
        [STAGE],
        3,
    )
    got = swap(away, BITS[0])

    cross_scratch = [pltpu.VMEM(SLOT_ROWS.shape, f32), FORCE_SCRATCH]
    for substep in range(2):
        first = substep == 0
        got_lead, got_trail = exchange(lead, trail, "gx")
        if not first:
            rows = call(
                inner_again,
                (SLOT_ROWS, SLOT_ROWS, FORCE_ROWS, FORCE_ROWS),
                (table, inner_pairs, hot_a, hot_b),
                cost=3,
            )
        lead, trail, side = call(
            pass_ghosts,
            (wide, wide, full_tile) if first else (narrow, narrow, single),
            (got_lead, got_trail, middle),
            after=(away,) if first else (rows[3],),
        )
        got_lead, got_trail = exchange(lead, trail, "gy")
        if first:
            stay, away = call(relay(0), (PARCELS, PARCELS), (stay, got), after=(lead, trail))
            got = swap(away, BITS[1])
            hot_a, hot_b, *rows = call(
                inner_start,
                (HOT, HOT, SLOT_ROWS, SLOT_ROWS, FORCE_ROWS, FORCE_ROWS),
                (table, inner_pairs),
                cost=3,
                after=(away,),
            )
            hot_c, hot_d, leading = call(
                cross_start, (HOT, HOT, SLOT_ROWS), (table, cross_pairs), after=(rows[3],)
            )
            on_crossing, lead, trail, side, reach = call(
                cross_kernel,
                (FORCE_ROWS, narrow, narrow, single, table_shape(SLOTS)),
                (leading, hot_d, got_lead, got_trail, side),
                cross_scratch,
                4,
            )
        else:
            leading = call(
                cross_again, SLOT_ROWS, (table, cross_pairs, hot_c), after=(lead, trail)
            )
            sums = call(inner_rest, (FORCE_ROWS, FORCE_ROWS), rows, cost=2, after=(leading,))
            on_crossing, lead, trail, side = call(
                cross_kernel_again,
                (FORCE_ROWS, narrow, narrow, single),
                (leading, hot_d, got_lead, got_trail, side, reach),
                cross_scratch,
                4,
                after=(sums[1],),
            )
        got_lead, got_trail = exchange(lead, trail, "gy")
        if first:
            stay, away = call(relay(1), (PARCELS, PARCELS), (stay, got), after=(side,))
            got = swap(away, BITS[2])
            sums = call(inner_rest, (FORCE_ROWS, FORCE_ROWS), rows, cost=2, after=(away,))
        force = call(
            scatter_kernel, three, (*sums, on_crossing, hot_a, hot_b, hot_c), cost=2, after=(side,)
        )
        if first:
            stay, away = call(relay(2), (PARCELS, PARCELS), (stay, got), after=(force,))
            got = swap(away, BITS[3])
        lead, trail, middle = call(
            pass_forces,
            (narrow, narrow, single),
            (got_lead, got_trail, side),
            after=(force, away) if first else (force,),
        )
        got_lead, got_trail = exchange(lead, trail, "gx")
        if first:
            at_grain, parcels = call(
                fluid_kernel,
                (full, jax.ShapeDtypeStruct((16, 8, LANES), f32)),
                (totals, stay, got, cells),
                [pltpu.VMEM((GROUP * LANES, LANES), f32)],
                3,
                after=(lead, trail),
            )
        else:
            fluid_out, void_out = call(
                owned_kernel,
                (like(fluid_velocity), table_shape(16, LANES)),
                (parcels, fluid, pressure),
                after=(lead, trail),
            )
        operands = (table, state, moving, at_grain, force, middle, got_lead, got_trail, hot)
        if first:
            table, state, moving, lead, trail, middle = call(
                middle_kernel, (full, full, three, narrow, narrow, single), operands
            )
        else:
            positions, velocity = call(
                last_kernel, (like(positions), like(positions)), operands, [STAGE]
            )
    return positions, velocity, fluid_out, void_out.reshape(-1)


def solution(mesh):
    placed = (
        P(None, ("gx", "gy")),
        P(None, ("gx", "gy")),
        P(("gx", "gy")),
        P(("gx", "gy")),
        P(("gx", "gy")),
        P(None, ("gx", "gy")),
        P(None, ("gx", "gy")),
        P(("gx", "gy")),
        P(None, ("gx", "gy")),
        P(None, ("gx", "gy")),
    )
    return jax.shard_map(
        shards,
        mesh=mesh,
        in_specs=placed,
        out_specs=(
            P(None, ("gx", "gy")),
            P(None, ("gx", "gy")),
            P(None, ("gx", "gy")),
            P(("gx", "gy")),
        ),
        check_vma=False,
    )
```

```python
import math

import jax
import jax.numpy as jnp
from jax import lax
from jax.experimental import pallas as pl
from jax.experimental.pallas import tpu as pltpu
from jax.sharding import PartitionSpec as P

SLOTS = 32
LANES = 128
CLUSTERS = 512
GHOSTS = 64
PAIRS = 1024
CHUNKS = 128
GROUP = 4
NEIGHBOURS = ((-1, -1), (-1, 0), (-1, 1), (0, -1), (0, 1), (1, -1), (1, 0), (1, 1))
GHOST_ORDER = (7, 2, 3, 4, 5, 0, 1, 6)
PAIRED = ("gx", "gy")
OTHER = {"gx": "gy", "gy": "gx"}
BITS = (1, 2, 4, 8)
FAR = 2.0**30

spring = 4.0
time_step = 0.1
grain_density = 2.65
gravity = 1.0
cell_volume = 4.0
void_floor = 0.35
drag_factor = 0.5

f32 = jnp.float32
bf16 = jnp.bfloat16
PARAMS = pltpu.CompilerParams(vmem_limit_bytes=24 * 1024 * 1024)


def split(values, parts):
    pieces = []
    for _ in range(parts - 1):
        piece = values.astype(bf16)
        pieces.append(piece)
        values = values - piece.astype(f32)
    pieces.append(values.astype(bf16))
    return pieces


def one_hot(index_row, count):
    width = index_row.shape[1]
    rows = lax.broadcasted_iota(jnp.int32, (LANES, width), 0).astype(f32).astype(bf16)
    blocks = []
    for k in range(count // LANES):
        within = index_row - k * LANES
        within = jnp.where((within >= 0) & (within < LANES), within, -1).astype(f32).astype(bf16)
        blocks.append(jnp.where(rows == within, jnp.ones((), bf16), jnp.zeros((), bf16)))
    return jnp.concatenate(blocks, axis=0) if len(blocks) > 1 else blocks[0]


def dot(left, right):
    return jnp.dot(left, right, preferred_element_type=f32)


def dot_lanes(left, right):
    return lax.dot_general(left, right, (((1,), (1,)), ((), ())), preferred_element_type=f32)


def cluster_column(index):
    return (index & (GROUP - 1)) * LANES + (index >> 2)


def ghost_column(slot):
    block = slot >> 6
    column = jnp.zeros_like(slot)
    for position, offset in enumerate(GHOST_ORDER):
        column = jnp.where(block == offset, position * GHOSTS, column)
    return column + (slot & (GHOSTS - 1))


def lower_half(shape):
    return lax.broadcasted_iota(jnp.int32, shape, 1) < GHOSTS


def swap_halves(tile):
    return jnp.concatenate([tile[:, GHOSTS:], tile[:, :GHOSTS]], axis=1)


def fold(whole, half, upper):
    rows = half.shape[0] // 2
    low = lower_half((rows, LANES))
    if upper:
        packed = jnp.where(low, swap_halves(half[:rows]), half[rows:])
    else:
        packed = jnp.where(low, half[:rows], swap_halves(half[rows:]))
    return jnp.concatenate([whole, packed], axis=0)


def unfold(folded, upper):
    rows = folded.shape[0] // 3
    packed = folded[2 * rows :]
    turned = swap_halves(packed)
    half = [turned, packed] if upper else [packed, turned]
    return folded[: 2 * rows], jnp.concatenate(half, axis=0)


def by_parity(axis, even_first, even_second):
    even = lax.axis_index(axis) % 2 == 0
    return (
        jnp.where(even, even_first, even_second),
        jnp.where(even, even_second, even_first),
    )


def outgoing(axis, up, down):
    if axis in PAIRED:
        return by_parity(axis, down, up)
    return by_parity(OTHER[axis], up, down)


def incoming(axis, lead, trail):
    return by_parity(axis if axis in PAIRED else OTHER[axis], lead, trail)


def to_table(square):
    turned = square.T
    return jnp.concatenate([turned[k * SLOTS : (k + 1) * SLOTS] for k in range(GROUP)], axis=1)


def from_table(table):
    stacked = jnp.concatenate([table[:, k * LANES : (k + 1) * LANES] for k in range(GROUP)], axis=0)
    return stacked.T


def load_components(ref, stage):
    for i in range(CHUNKS):
        stage[pl.ds(i, 3, stride=CHUNKS), :] = ref[:, i * LANES : (i + 1) * LANES]
    return [to_table(stage[c * CHUNKS : (c + 1) * CHUNKS, :]) for c in range(3)]


def store_components(ref, stage, table):
    for c in range(3):
        stage[c * CHUNKS : (c + 1) * CHUNKS, :] = from_table(table[c * SLOTS : (c + 1) * SLOTS])
    for i in range(CHUNKS):
        ref[:, i * LANES : (i + 1) * LANES] = stage[pl.ds(i, 3, stride=CHUNKS), :]


def gather(table_parts, hot, rows):
    picked = dot(table_parts, hot)
    total = picked[:rows]
    for k in range(1, table_parts.shape[0] // rows):
        total = total + picked[k * rows : (k + 1) * rows]
    return total


def send_pieces(table, rows, hot, lead, trail, middle):
    pieces = gather(table_parts(table[:rows]), hot[...], rows)
    tiles = [pieces[:, k * LANES : (k + 1) * LANES] for k in range(4)]
    up = fold(tiles[3], tiles[2], True)
    down = fold(tiles[0], tiles[1], False)
    lead[...], trail[...] = outgoing("gx", up, down)
    middle[...] = jnp.where(lower_half(tiles[1].shape), tiles[2], tiles[1])


def start_copies(pairs, arrived, first=0):
    copies = [
        pltpu.make_async_copy(far, near, arrived.at[first + k])
        for k, (far, near) in enumerate(pairs)
    ]
    for copy in copies:
        copy.start()
    return copies


def prepare(
    positions_far, radius_far, mask_far, send_far,
    velocity_far, cell_far, fluid_far, pressure_far, inner_far, cross_far,
    table_out, state_out, hot, lead, trail, middle, velocity, cell, fluid, pressure, inner, cross,
    positions, radius, mask, send, stage, arrived,
):
    needed = start_copies(
        ((positions_far, positions), (radius_far, radius), (mask_far, mask), (send_far, send)), arrived
    )
    later = start_copies(
        (
            (velocity_far, velocity),
            (cell_far, cell),
            (fluid_far, fluid),
            (pressure_far, pressure),
            (inner_far, inner),
            (cross_far, cross),
        ),
        arrived,
        4,
    )
    for copy in needed:
        copy.wait()
    parts = load_components(positions, stage)
    reach = to_table(radius[...])
    weights = to_table(mask[...].astype(f32))
    real = weights > 0.5
    table = jnp.concatenate([jnp.where(real, part, FAR) for part in parts] + [reach], axis=0)
    table_out[...] = table
    for c in range(3):
        state_out[c * SLOTS : (c + 1) * SLOTS] = parts[c]
    state_out[3 * SLOTS :] = weights
    hot[...] = one_hot(cluster_column(send[...]), CLUSTERS)
    send_pieces(table, 4 * SLOTS, hot, lead, trail, middle)
    for copy in later:
        copy.wait()


def contacts(leading, partner, on_leading, on_partner, begin, end):
    step = 4

    def row(component, slot):
        return pl.ds(pl.multiple_of((component * SLOTS + slot) * 8, 8), 8)

    def some_slots(block, carry):
        base = block * step
        ours = [[leading[row(c, base + i), :] for c in range(4)] for i in range(step)]
        sums = [[jnp.zeros((8, LANES), f32) for _ in range(3)] for _ in range(step)]
        for q in range(SLOTS):
            theirs = [partner[row(c, q), :] for c in range(4)]
            back = [on_partner[row(c, q), :] for c in range(3)]
            for i in range(step):
                apart = [ours[i][c] - theirs[c] for c in range(3)]
                squared = apart[0] * apart[0] + apart[1] * apart[1] + apart[2] * apart[2]
                reach = ours[i][3] + theirs[3]
                weight = jnp.maximum(reach * reach - squared, 0.0)
                for c in range(3):
                    push = weight * apart[c]
                    sums[i][c] = sums[i][c] + push
                    back[c] = back[c] + push
            for c in range(3):
                on_partner[row(c, q), :] = back[c]
        for i in range(step):
            for c in range(3):
                on_leading[row(c, base + i), :] = sums[i][c]
        return carry

    lax.fori_loop(begin // step, end // step, some_slots, 0)


def fill_hot(pairs, row, column, hot):
    width = 2 * LANES
    for block in range(PAIRS // width):
        span = slice(block * width, (block + 1) * width)
        hot[:, span] = one_hot(column(pairs[row : row + 1, span]), CLUSTERS)


def fill_slots(parts, hot, pairs, landed):
    width = 2 * LANES
    for block in range(PAIRS // width):
        span = slice(block * width, (block + 1) * width)
        picked = gather(parts, hot[:, span], 4 * SLOTS)
        if pairs is not None:
            offsets = pairs[2:5, span].astype(f32)
            picked = jnp.concatenate(
                [picked[c * SLOTS : (c + 1) * SLOTS] - offsets[c : c + 1] for c in range(3)]
                + [picked[3 * SLOTS :]],
                axis=0,
            )
        for k in range(2):
            landed[pl.ds(2 * block + k, 4 * SLOTS, stride=8), :] = picked[
                :, k * LANES : (k + 1) * LANES
            ]


def scatter(*terms):
    parts, hots = [], []
    for sums, hot, sign in terms:
        pieces = jnp.concatenate(
            [sums[pl.ds(k, 3 * SLOTS, stride=8), :] for k in range(PAIRS // LANES)], axis=1
        )
        parts.append(jnp.concatenate(split(pieces if sign > 0 else -pieces, 2), axis=0))
        hots.append(hot[...])
    added = dot_lanes(jnp.concatenate(parts, axis=1), jnp.concatenate(hots, axis=1))
    return added[: 3 * SLOTS] + added[3 * SLOTS :]


def table_parts(table):
    return jnp.concatenate(split(table[...], 2), axis=0)


INNER_SPLIT = 16


def inner_start(table, pairs, hot_a, hot_b, leading, partner, on_leading, on_partner):
    fill_hot(pairs, 0, cluster_column, hot_a)
    fill_hot(pairs, 1, cluster_column, hot_b)
    inner_again(table, pairs, hot_a, hot_b, leading, partner, on_leading, on_partner)


def inner_again(table, pairs, hot_a, hot_b, leading, partner, on_leading, on_partner):
    parts = table_parts(table)
    fill_slots(parts, hot_a, pairs, leading)
    fill_slots(parts, hot_b, None, partner)
    on_partner[...] = jnp.zeros_like(on_partner)
    contacts(leading, partner, on_leading, on_partner, 0, INNER_SPLIT)
    for c in range(3):
        later = slice((c * SLOTS + INNER_SPLIT) * 8, (c + 1) * SLOTS * 8)
        on_leading[later, :] = jnp.zeros(((SLOTS - INNER_SPLIT) * 8, LANES), f32)


def inner_rest(leading, partner, on_leading_first, on_partner_first, on_leading, on_partner):
    for c in range(3):
        done = slice(c * SLOTS * 8, (c * SLOTS + INNER_SPLIT) * 8)
        on_leading[done, :] = on_leading_first[done, :]
    on_partner[...] = on_partner_first[...]
    contacts(leading, partner, on_leading, on_partner, INNER_SPLIT, SLOTS)


def cross_start(table, pairs, hot_a, hot_b, leading):
    fill_hot(pairs, 0, cluster_column, hot_a)
    fill_hot(pairs, 1, ghost_column, hot_b)
    cross_again(table, pairs, hot_a, leading)


def cross_again(table, pairs, hot_a, leading):
    fill_slots(table_parts(table), hot_a, pairs, leading)


def scatter_kernel(on_leading, on_partner, on_crossing, hot_a, hot_b, hot_c, force):
    force[...] = scatter((on_leading, hot_a, 1), (on_partner, hot_b, -1), (on_crossing, hot_c, 1))


def present_tile(low, high):
    here_x, here_y = lax.axis_index("gx"), lax.axis_index("gy")
    flags = []
    for slot in (low, high):
        a, b = NEIGHBOURS[slot]
        x, y = here_x + a, here_y + b
        inside = (x >= 0) & (x < lax.axis_size("gx")) & (y >= 0) & (y < lax.axis_size("gy"))
        flags.append(jnp.where(inside, 1, 0))
    return jnp.where(lower_half((1, LANES)), flags[0], flags[1]) > 0


def pass_ghosts(got_lead, got_trail, middle, lead_out, trail_out, side):
    low = lower_half(middle.shape)
    from_last, from_next = incoming("gx", got_lead[...], got_trail[...])
    last_whole, last_half = unfold(from_last, True)
    next_whole, next_half = unfold(from_next, False)
    minus = fold(jnp.where(low, next_whole, last_half), middle[...], True)
    plus = fold(jnp.where(low, next_half, last_whole), middle[...], False)
    lead_out[...], trail_out[...] = outgoing("gy", plus, minus)
    side[...] = jnp.where(low, last_whole, next_whole)


def cross_contacts(ghosts, leading, hot_b, on_leading, lead, trail, side_out, partner, on_partner):
    fill_slots(table_parts(ghosts), hot_b, None, partner)
    on_partner[...] = jnp.zeros_like(on_partner)
    contacts(leading, partner, on_leading, on_partner, 0, SLOTS)
    back = scatter((on_partner, hot_b, 1))
    tiles = [back[:, k * LANES : (k + 1) * LANES] for k in range(4)]
    up = fold(tiles[0], tiles[1], True)
    down = fold(tiles[2], tiles[1], False)
    lead[...], trail[...] = outgoing("gy", up, down)
    side_out[...] = tiles[3]


def ghost_places(got_lead, got_trail, side):
    from_last, from_next = incoming("gy", got_lead[...], got_trail[...])
    last_whole, last_half = unfold(from_last, False)
    next_whole, next_half = unfold(from_next, True)
    low = lower_half(side.shape)
    tiles = [next_whole, jnp.where(low, last_half, next_half), last_whole, side[...]]
    placed = [
        jnp.where(
            present_tile(GHOST_ORDER[2 * k], GHOST_ORDER[2 * k + 1]), tiles[k][: 3 * SLOTS], FAR
        )
        for k in range(4)
    ]
    return tiles, jnp.concatenate(placed, axis=1)


def cross_kernel(
    leading, hot_b, got_lead, got_trail, side,
    on_leading, lead, trail, side_out, reach_out, partner, on_partner,
):
    tiles, placed = ghost_places(got_lead, got_trail, side)
    reach = jnp.concatenate([tile[3 * SLOTS :] for tile in tiles], axis=1)
    reach_out[...] = reach
    ghosts = jnp.concatenate([placed, reach], axis=0)
    cross_contacts(ghosts, leading, hot_b, on_leading, lead, trail, side_out, partner, on_partner)


def cross_kernel_again(
    leading, hot_b, got_lead, got_trail, side, reach,
    on_leading, lead, trail, side_out, partner, on_partner,
):
    _, placed = ghost_places(got_lead, got_trail, side)
    ghosts = jnp.concatenate([placed, reach[...]], axis=0)
    cross_contacts(ghosts, leading, hot_b, on_leading, lead, trail, side_out, partner, on_partner)


def pass_forces(got_lead, got_trail, side, lead_out, trail_out, middle):
    low = lower_half((3 * SLOTS, LANES))
    from_last, from_next = incoming("gy", got_lead[...], got_trail[...])
    last_whole, last_half = unfold(from_last, True)
    next_whole, next_half = unfold(from_next, False)
    up = fold(jnp.where(low, last_whole, side[...]), next_whole, False)
    down = fold(jnp.where(low, side[...], next_whole), last_whole, True)
    lead_out[...], trail_out[...] = outgoing("gx", up, down)
    middle[...] = jnp.where(low, next_half, last_half)


def part_parcels(parcels, bit, stay, away):
    mine = (lax.axis_index("gy") & bit) > 0
    for k, low in enumerate([d for d in range(16) if not d & bit]):
        stay[k] = jnp.where(mine, parcels[low | bit], parcels[low])
        away[k] = jnp.where(mine, parcels[low], parcels[low | bit])


def join_parcels(stay, got, bit):
    mine = (lax.axis_index("gy") & bit) > 0
    parcels = [None] * 16
    for k, low in enumerate([d for d in range(16) if not d & bit]):
        parcels[low] = jnp.where(mine, got[k], stay[k])
        parcels[low | bit] = jnp.where(mine, stay[k], got[k])
    return parcels


def relay(step):
    def relay_parcels(stay, got, stay_out, away_out):
        part_parcels(join_parcels(stay, got, BITS[step]), BITS[step + 1], stay_out, away_out)

    return relay_parcels


def deposit_kernel(
    table, state, velocity, cell, fluid, pressure, velocity_out, cell_out, totals_out, stay, away, stage
):
    parts = load_components(velocity, stage)
    reach = table[3 * SLOTS :, :]
    weights = state[3 * SLOTS :, :]
    cells = to_table(cell[...].astype(f32)).astype(jnp.int32)
    volumes = weights * ((4.0 * math.pi / 3.0) * reach * reach * reach)
    for c in range(3):
        velocity_out[c * SLOTS : (c + 1) * SLOTS] = parts[c]
    cell_out[...] = cells
    amounts = [volumes] + [volumes * part for part in parts]
    highs = [amount.astype(bf16).astype(f32) for amount in amounts]
    lows = [amount - high for amount, high in zip(amounts, highs)]
    rows = lax.broadcasted_iota(jnp.int32, (16, CLUSTERS), 0).astype(f32).astype(bf16)
    total = jnp.zeros((2 * 4 * 16, LANES), f32)
    for slot in range(SLOTS):
        cell_row = cells[slot : slot + 1]
        hot = one_hot(cell_row & (LANES - 1), LANES)
        group = rows == (cell_row >> 7).astype(f32).astype(bf16)
        spread = [
            jnp.where(group, part[slot : slot + 1].astype(bf16), jnp.zeros((), bf16))
            for part in highs + lows
        ]
        total = total + dot_lanes(jnp.concatenate(spread, axis=0), hot)
    total = total[:64] + total[64:]
    totals_out[...] = total
    parcels = []
    for owner in range(16):
        span = slice(owner * LANES, (owner + 1) * LANES)
        parcels.append(
            jnp.concatenate(
                [total[c * 16 + owner : c * 16 + owner + 1] for c in range(4)]
                + [fluid[:, span] + time_step * pressure[:, span], jnp.zeros((1, LANES), f32)],
                axis=0,
            )
        )
    part_parcels(parcels, BITS[0], stay, away)


def fluid_kernel(totals, stay, got, cell, at_grain, parcels_out, stage):
    parcels = join_parcels(stay, got, BITS[3])
    for source in range(16):
        parcels_out[source] = parcels[source]
    volume = totals[:16]
    void_here = jnp.maximum(1.0 - volume / cell_volume, void_floor)
    drag_rate = drag_factor * (1.1 - void_here) / (void_here * void_here)
    below = void_here + time_step * drag_rate * volume / cell_volume
    fields = []
    for c in range(3):
        momentum = drag_rate * totals[(c + 1) * 16 : (c + 2) * 16] / cell_volume
        driven = jnp.concatenate([parcels[k][4 + c : 5 + c] for k in range(16)], axis=0)
        fields.append((void_here * driven + time_step * momentum) / below)
    fields.append(drag_rate)
    mixed = jnp.concatenate(
        [field[k : k + 1] for k in range(16) for field in fields], axis=0
    )
    parts = jnp.concatenate(split(mixed, 2), axis=0)
    ranges = lax.broadcasted_iota(jnp.int32, (64, CLUSTERS), 0) >> 2
    for slot in range(SLOTS):
        cell_row = cell[slot : slot + 1, :]
        seen = dot(parts, one_hot(cell_row & (LANES - 1), LANES))
        chosen = jnp.where(ranges == (cell_row >> 7), seen[:64] + seen[64:], 0.0)
        found = chosen[:8]
        for k in range(1, 8):
            found = found + chosen[8 * k : 8 * (k + 1)]
        found = found[:4] + found[4:]
        for k in range(GROUP):
            row = k * LANES + slot * 4
            stage[row : row + 4, :] = found[:, k * LANES : (k + 1) * LANES]
    for c in range(4):
        for k in range(GROUP):
            at_grain[c * SLOTS : (c + 1) * SLOTS, k * LANES : (k + 1) * LANES] = stage[
                pl.ds(k * LANES + c, SLOTS, stride=4), :
            ]


def owned_kernel(parcels, fluid, pressure, fluid_out, void_out):
    for source in range(16):
        span = slice(source * LANES, (source + 1) * LANES)
        volume = parcels[source, 0:1, :]
        void_here = jnp.maximum(1.0 - volume / cell_volume, void_floor)
        drag_rate = drag_factor * (1.1 - void_here) / (void_here * void_here)
        below = void_here + time_step * drag_rate * volume / cell_volume
        push = void_here * pressure[:, span] + drag_rate * parcels[source, 1:4, :] / cell_volume
        fluid_out[:, span] = (void_here * fluid[:, span] + time_step * push) / below
        void_out[source : source + 1, :] = void_here


def advance(state, velocity, reach, at_grain, force, middle, got_lead, got_trail, hot):
    low = lower_half((3 * SLOTS, LANES))
    from_last, from_next = incoming("gx", got_lead[...], got_trail[...])
    last_whole, last_half = unfold(from_last, False)
    next_whole, next_half = unfold(from_next, True)
    tiles = [
        last_whole,
        jnp.where(low, last_half, middle[...]),
        jnp.where(low, middle[...], next_half),
        next_whole,
    ]
    tiles = [jnp.where(present_tile(2 * k, 2 * k + 1), tiles[k], 0.0) for k in range(4)]
    returned = jnp.concatenate(tiles, axis=1)
    added = dot_lanes(jnp.concatenate(split(returned, 2), axis=0), hot[...])
    contact = spring * (force[...] - (added[: 3 * SLOTS] + added[3 * SLOTS :]))
    weights = state[3 * SLOTS :, :]
    sphere = (4.0 * math.pi / 3.0) * reach * reach * reach
    masses = grain_density * sphere
    volumes = weights * sphere
    drag = at_grain[3 * SLOTS :, :] * volumes
    places, speeds = [], []
    for c in range(3):
        rows = slice(c * SLOTS, (c + 1) * SLOTS)
        speed = velocity[rows, :]
        pull = (contact[rows] + drag * (at_grain[rows, :] - speed)) / masses
        if c == 2:
            pull = pull - gravity
        speed = speed + time_step * weights * pull
        speeds.append(speed)
        places.append(state[rows, :] + time_step * weights * speed)
    return places, speeds, weights


def middle_kernel(
    table, state, velocity, at_grain, force, middle, got_lead, got_trail, hot,
    table_out, state_out, velocity_out, lead, trail, middle_out,
):
    reach = table[3 * SLOTS :, :]
    places, speeds, weights = advance(
        state, velocity, reach, at_grain, force, middle, got_lead, got_trail, hot
    )
    real = weights > 0.5
    moved = jnp.concatenate([jnp.where(real, place, FAR) for place in places] + [reach], axis=0)
    table_out[...] = moved
    for c in range(3):
        state_out[c * SLOTS : (c + 1) * SLOTS] = places[c]
        velocity_out[c * SLOTS : (c + 1) * SLOTS] = speeds[c]
    state_out[3 * SLOTS :] = weights
    send_pieces(moved, 3 * SLOTS, hot, lead, trail, middle_out)


def last_kernel(
    table, state, velocity, at_grain, force, middle, got_lead, got_trail, hot,
    positions_out, velocity_out, stage,
):
    places, speeds, _ = advance(
        state, velocity, table[3 * SLOTS :, :], at_grain, force, middle, got_lead, got_trail, hot
    )
    store_components(positions_out, stage, jnp.concatenate(places, axis=0))
    store_components(velocity_out, stage, jnp.concatenate(speeds, axis=0))


def exchange(lead, trail, axis):
    size_x, size_y = lax.axis_size("gx"), lax.axis_size("gy")
    routes = ([], [])
    for x in range(size_x):
        for y in range(size_y):
            along, across = (x, y) if axis == "gx" else (y, x)
            last = (size_x if axis == "gx" else size_y) - 1
            up_first = along % 2 == 1 if axis in PAIRED else across % 2 == 0
            for route, step in zip(routes, (1, -1) if up_first else (-1, 1)):
                target = along + step
                ends = (target, across) if 0 <= target <= last else (along, across ^ 1)
                to_x, to_y = ends if axis == "gx" else ends[::-1]
                route.append((x * size_y + y, to_x * size_y + to_y))
    return tuple(
        lax.ppermute(block, ("gx", "gy"), route) for block, route in zip((lead, trail), routes)
    )


def swap(array, bit):
    size_x, size_y = lax.axis_size("gx"), lax.axis_size("gy")
    moves = [(x * size_y + y, x * size_y + (y ^ bit)) for x in range(size_x) for y in range(size_y)]
    return lax.ppermute(array, ("gx", "gy"), moves)


def table_shape(rows, columns=CLUSTERS):
    return jax.ShapeDtypeStruct((rows, columns), f32)


STAGE = pltpu.VMEM((3 * CHUNKS, LANES), f32)
HOT = jax.ShapeDtypeStruct((CLUSTERS, PAIRS), bf16)
SLOT_ROWS = table_shape(4 * SLOTS * 8, LANES)
FORCE_ROWS = table_shape(3 * SLOTS * 8, LANES)
FORCE_SCRATCH = pltpu.VMEM((3 * SLOTS * 8, LANES), f32)
PARCELS = jax.ShapeDtypeStruct((8, 8, LANES), f32)


def call(kernel, out_shape, operands, scratch=(), cost=1.0, far=False, after=()):
    count = len(operands)

    def body(*refs):
        kernel(*refs[:count], *refs[count + len(after) :])

    space = pltpu.HBM if far else pltpu.VMEM
    if far:
        operands = tuple(pltpu.with_memory_space_constraint(array, pltpu.HBM) for array in operands)
    return pl.pallas_call(
        body,
        out_shape=out_shape,
        in_specs=[pl.BlockSpec(memory_space=space)] * count
        + [pl.BlockSpec(memory_space=pl.ANY)] * len(after),
        scratch_shapes=list(scratch),
        compiler_params=PARAMS,
        cost_estimate=pl.CostEstimate(
            flops=int(cost * 10**9), bytes_accessed=int(cost * 10**6), transcendentals=0
        ),
        name=kernel.__name__,
    )(*operands, *after)


def shards(
    positions,
    velocity,
    radius,
    grain_mask,
    grain_cell,
    inner_pairs,
    cross_pairs,
    send_lists,
    fluid_velocity,
    pressure_grad,
):
    send = send_lists.reshape(1, -1)
    radius = radius.reshape(CHUNKS, LANES)
    mask = grain_mask.reshape(CHUNKS, LANES)
    cell = grain_cell.reshape(CHUNKS, LANES)

    full, wide = table_shape(4 * SLOTS), table_shape(6 * SLOTS, LANES)
    narrow, single = table_shape(9 * SLOTS // 2, LANES), table_shape(3 * SLOTS, LANES)
    three, full_tile = table_shape(3 * SLOTS), table_shape(4 * SLOTS, LANES)

    def near(array):
        return pltpu.VMEM(array.shape, array.dtype)

    def like(array):
        return jax.ShapeDtypeStruct(array.shape, array.dtype)

    needed = (positions, radius, mask, send)
    later = (velocity, cell, fluid_velocity, pressure_grad, inner_pairs, cross_pairs)
    table, state, hot, lead, trail, middle, *later = call(
        prepare,
        (
            full,
            full,
            jax.ShapeDtypeStruct((CLUSTERS, CLUSTERS), bf16),
            wide,
            wide,
            full_tile,
            *[like(array) for array in later],
        ),
        needed + later,
        [near(array) for array in needed] + [STAGE, pltpu.SemaphoreType.DMA((10,))],
        far=True,
    )
    velocity, cell, fluid, pressure, inner_pairs, cross_pairs = later
    moving, cells, totals, stay, away = call(
        deposit_kernel,
        (
            three,
            jax.ShapeDtypeStruct((SLOTS, CLUSTERS), jnp.int32),
            table_shape(64, LANES),
            PARCELS,
            PARCELS,
        ),
        (table, state, velocity, cell, fluid, pressure),
        [STAGE],
        3,
    )
    got = swap(away, BITS[0])

    cross_scratch = [pltpu.VMEM(SLOT_ROWS.shape, f32), FORCE_SCRATCH]
    for substep in range(2):
        first = substep == 0
        got_lead, got_trail = exchange(lead, trail, "gx")
        if not first:
            rows = call(
                inner_again,
                (SLOT_ROWS, SLOT_ROWS, FORCE_ROWS, FORCE_ROWS),
                (table, inner_pairs, hot_a, hot_b),
                cost=3,
            )
        if first:
            hot_c, hot_d, leading = call(
                cross_start, (HOT, HOT, SLOT_ROWS), (table, cross_pairs), after=(away,)
            )
        lead, trail, side = call(
            pass_ghosts,
            (wide, wide, full_tile) if first else (narrow, narrow, single),
            (got_lead, got_trail, middle),
            after=(leading,) if first else (rows[3],),
        )
        got_lead, got_trail = exchange(lead, trail, "gy")
        if first:
            stay, away = call(relay(0), (PARCELS, PARCELS), (stay, got), after=(lead, trail))
            got = swap(away, BITS[1])
            hot_a, hot_b, *rows = call(
                inner_start,
                (HOT, HOT, SLOT_ROWS, SLOT_ROWS, FORCE_ROWS, FORCE_ROWS),
                (table, inner_pairs),
                cost=3,
                after=(away,),
            )
            on_crossing, lead, trail, side, reach = call(
                cross_kernel,
                (FORCE_ROWS, narrow, narrow, single, table_shape(SLOTS)),
                (leading, hot_d, got_lead, got_trail, side),
                cross_scratch,
                4,
            )
        else:
            leading = call(
                cross_again, SLOT_ROWS, (table, cross_pairs, hot_c), after=(lead, trail)
            )
            sums = call(inner_rest, (FORCE_ROWS, FORCE_ROWS), rows, cost=2, after=(leading,))
            on_crossing, lead, trail, side = call(
                cross_kernel_again,
                (FORCE_ROWS, narrow, narrow, single),
                (leading, hot_d, got_lead, got_trail, side, reach),
                cross_scratch,
                4,
                after=(sums[1],),
            )
        got_lead, got_trail = exchange(lead, trail, "gy")
        if first:
            stay, away = call(relay(1), (PARCELS, PARCELS), (stay, got), after=(side,))
            got = swap(away, BITS[2])
            sums = call(inner_rest, (FORCE_ROWS, FORCE_ROWS), rows, cost=2, after=(away,))
            stay, away = call(relay(2), (PARCELS, PARCELS), (stay, got), after=(sums[1],))
            got = swap(away, BITS[3])
        force = call(
            scatter_kernel,
            three,
            (*sums, on_crossing, hot_a, hot_b, hot_c),
            cost=2,
            after=(side, away) if first else (side,),
        )
        lead, trail, middle = call(
            pass_forces,
            (narrow, narrow, single),
            (got_lead, got_trail, side),
            after=(force,),
        )
        got_lead, got_trail = exchange(lead, trail, "gx")
        if first:
            at_grain, parcels = call(
                fluid_kernel,
                (full, jax.ShapeDtypeStruct((16, 8, LANES), f32)),
                (totals, stay, got, cells),
                [pltpu.VMEM((GROUP * LANES, LANES), f32)],
                3,
                after=(lead, trail),
            )
        else:
            fluid_out, void_out = call(
                owned_kernel,
                (like(fluid_velocity), table_shape(16, LANES)),
                (parcels, fluid, pressure),
                after=(lead, trail),
            )
        operands = (table, state, moving, at_grain, force, middle, got_lead, got_trail, hot)
        if first:
            table, state, moving, lead, trail, middle = call(
                middle_kernel, (full, full, three, narrow, narrow, single), operands
            )
        else:
            positions, velocity = call(
                last_kernel, (like(positions), like(positions)), operands, [STAGE]
            )
    return positions, velocity, fluid_out, void_out.reshape(-1)


def solution(mesh):
    placed = (
        P(None, ("gx", "gy")),
        P(None, ("gx", "gy")),
        P(("gx", "gy")),
        P(("gx", "gy")),
        P(("gx", "gy")),
        P(None, ("gx", "gy")),
        P(None, ("gx", "gy")),
        P(("gx", "gy")),
        P(None, ("gx", "gy")),
        P(None, ("gx", "gy")),
    )
    return jax.shard_map(
        shards,
        mesh=mesh,
        in_specs=placed,
        out_specs=(
            P(None, ("gx", "gy")),
            P(None, ("gx", "gy")),
            P(None, ("gx", "gy")),
            P(("gx", "gy")),
        ),
        check_vma=False,
    )
```
